256 devices in a mesh: macro: 32 (over z, y), pencil: 8 (over x, core).
Axes of the slice: x: 4, y: 4, z: 8, core: 2. Of those that a mesh axis runs over, the one named last changes fastest.
Arguments:
- voxel_material_ids: int32 [32, 128, 128, 128], P('macro', 'pencil'), may hold values from 0 to 2
- fiber_fraction: float32 [32, 128, 128, 128], P('macro', 'pencil'), may hold values from 0.5 to 18, as said below
- material_matrix_diffusivity: float32 [32, 3], P('macro'), may hold values from 0.2 to 5
- mesh_point_thermal_state: float32 [128], P('macro'), may hold values from 0.5 to 1.5
- element_corner_ids: int32 [32, 8], P('macro'), may hold values from 0 to 127, all different within a row
- global_entry_position: int32 [128], P('macro'), may hold values from 0 to 127, each once
- sample_choice_per_point: int32 [32], P('macro'), may hold values from 0 to 31, as said below
Outputs:
- qp_flux: float32 [32, 3], P('macro')
- nodal_flux: float32 [128], P('macro')
The draws below stay inside these ranges and needn't reach their ends.
Inputs may be any that keep to these rules, and one draw needn't show every extreme that they name: `fiber_fraction`: positive. `sample_choice_per_point`: exactly 8 microstructures are used by 2 points each, 16 by 1 points each, and the rest by none.
All inputs are finite; a program needn't handle non-finite values.
Results may differ from the reference program's by a relative error of at most 0.0003.
Values sent between devices are 32-bit elements; how exact they have to be, the bound alone decides.
No kernel may reach another device: no remote copies, remote signals or barrier semaphores. Data moves between devices by JAX's collectives and lax.ppermute only.
A program may use at most 64 MiB of HBM per device.

```python
import math
import jax
import jax.numpy as jnp
from jax import lax

NV = 128
PHASES = 3
ITERS = 2
QP_DEV = 1
MICRO = 32
QPS = 32
GLOBAL_MESH_PTS = 128


def draw_fiber_fraction(key, part):
    key_base, key_cols = jax.random.split(jax.random.fold_in(key, 7))
    shape = (MICRO, NV, NV, NV)
    base = jnp.exp(jax.random.uniform(key_base, shape, jnp.float32, math.log(0.5), math.log(2.0)))
    cols = jnp.exp(jax.random.uniform(key_cols, (MICRO, 1, NV, 1), jnp.float32, 0.0, math.log(3.0)))
    ramp = jnp.exp(math.log(3.0) * jnp.arange(NV).astype(jnp.float32) / (NV - 1)).reshape(1, NV, 1, 1)
    return (base * cols * ramp).astype(jnp.float32)


def draw_sample_choice_per_point(key, part):
    key_groups, key_points = jax.random.split(jax.random.fold_in(key, 11))
    order = jax.random.permutation(key_groups, MICRO)
    places = jnp.arange(QPS)
    quarter = MICRO // 4
    heavy_index = jnp.clip(places // (2 * QP_DEV), 0, quarter - 1)
    light_index = jnp.clip(quarter + (places - QPS // 2) // QP_DEV, 0, MICRO - 1)
    group = jnp.where(places < QPS // 2, order[heavy_index], order[light_index])
    return jax.random.permutation(key_points, group).astype(jnp.int32)


def place_ends(values, own_key, smallest, high):
    place = [jax.random.randint(jax.random.fold_in(own_key, axis), (), 0, length) for axis, length in enumerate(values.shape)]
    main_axis = values.shape.index(max(values.shape))
    neighbour = place[:main_axis] + [(place[main_axis] + 1) % values.shape[main_axis]] + place[main_axis + 1:]
    return values.at[tuple(place)].set(smallest).at[tuple(neighbour)].set(high)


def block_levels(stream_key, dims, cuts, smallest, largest):
    gain, own = 1.0, jax.random.fold_in(stream_key, 6)
    for axis_at, blocks in cuts:
        steps = jnp.exp(jax.random.uniform(jax.random.fold_in(own, axis_at), (blocks,), jnp.float32, smallest / len(cuts), largest / len(cuts)))
        gain = gain * jnp.repeat(steps, dims[axis_at] // blocks).reshape([-1 if axis == axis_at else 1 for axis in range(len(dims))])
    return gain


def choose_distinct(stream_key, rows, count, top, lift):
    sequence = jax.random.permutation(jax.random.fold_in(stream_key, 1), count)
    favour = sequence
    for power in range(3):
        favour = favour * favour // count
    favour = favour * lift // count
    tickets = jax.random.randint(jax.random.fold_in(stream_key, 2), (rows, count), 0, 4096) + favour
    fixed_rows = jax.random.permutation(jax.random.fold_in(stream_key, 3), rows)[jnp.arange(count) % rows]
    tickets = jnp.where(jnp.arange(rows)[:, None] == fixed_rows[None, :], 1 << 14, tickets)
    merit = tickets * count + jnp.arange(count)
    return lax.top_k(merit.astype(jnp.int32), top)[1].astype(jnp.int32)


def setup_inputs(seed: int = 0) -> dict:
    streams_of = jax.random.split(jax.random.key(seed), 8)
    return {
        "voxel_material_ids": place_ends(jax.random.randint(streams_of[0], (MICRO, NV, NV, NV), 0, PHASES), jax.random.fold_in(streams_of[0], 1), 0, PHASES - 1).astype(jnp.int32),
        "fiber_fraction": draw_fiber_fraction(jax.random.fold_in(streams_of[7], 71), 0),
        "material_matrix_diffusivity": jnp.clip(jnp.exp(math.log(5.0) - 3.218876 * jax.random.uniform(streams_of[2], (MICRO, PHASES), jnp.float32) ** block_levels(streams_of[2], (MICRO, PHASES), ((0, 32),), -0.2, 0.2)), 0.2, 5.0),
        "mesh_point_thermal_state": jnp.clip(0.5 + 1.0 * jax.random.uniform(streams_of[3], (GLOBAL_MESH_PTS,), jnp.float32) ** block_levels(streams_of[3], (GLOBAL_MESH_PTS,), ((0, 32),), -0.2, 0.2), 0.5, 1.5),
        "element_corner_ids": choose_distinct(streams_of[4], QPS, GLOBAL_MESH_PTS, 8, 0),
        "global_entry_position": jax.random.permutation(streams_of[5], GLOBAL_MESH_PTS).astype(jnp.int32),
        "sample_choice_per_point": draw_sample_choice_per_point(jax.random.fold_in(streams_of[7], 71), 0),
    }


HIGHEST = lax.Precision.HIGHEST

def corner_signs():
    table = [[2.0 * (corner >> device_axis & 1) - 1.0 for device_axis in range(3)] for corner in range(8)]
    return jnp.array(table, dtype=jnp.float32)

def base_field(voxel_material_ids, fiber_fraction, material_matrix_diffusivity):
    conduct = jnp.zeros(fiber_fraction.shape, jnp.float32)
    for phase in range(PHASES):
        column = material_matrix_diffusivity[:, phase][:, None, None, None]
        conduct = conduct + jnp.where(voxel_material_ids == phase, column, 0.0)
    return conduct * fiber_fraction

def solve_point(conduct, gradient, heat):
    field = conduct + heat ** 3
    reference_k = jnp.sqrt(jnp.mean(field * field))
    modes = jnp.arange(NV).astype(jnp.float32)
    line = 4.0 * jnp.sin(math.pi * modes / NV) ** 2
    eigen = line[:, None, None] + line[None, :, None] + line[None, None, :]
    positive = eigen > 0
    weight = jnp.where(positive, 1.0 / (reference_k * jnp.where(positive, eigen, 1.0)), 0.0)
    gradient_field = [gradient[device_axis] + jnp.zeros_like(field) for device_axis in range(3)]
    for sweep in range(ITERS):
        source = jnp.zeros_like(field)
        for device_axis in range(3):
            polar = (field - reference_k) * gradient_field[device_axis]
            source = source + polar - jnp.roll(polar, 1, axis=device_axis)
        potential = jnp.real(jnp.fft.ifftn(jnp.fft.fftn(source) * weight))
        gradient_field = [gradient[device_axis] + jnp.roll(potential, -1, axis=device_axis) - potential for device_axis in range(3)]
    return jnp.stack([jnp.mean(field * gradient_field[device_axis]) for device_axis in range(3)])

def reference(voxel_material_ids, fiber_fraction, material_matrix_diffusivity, mesh_point_thermal_state, element_corner_ids, global_entry_position, sample_choice_per_point):
    signs = corner_signs()
    fourier_argument = mesh_point_thermal_state[element_corner_ids]
    gradient = jnp.dot(fourier_argument, signs, precision=HIGHEST) / 4.0
    heat = lax.optimization_barrier(jnp.sum(fourier_argument, axis=1)) / 8.0
    conduct = base_field(voxel_material_ids, fiber_fraction, material_matrix_diffusivity)

    def one_point(packed):
        point_gradient, point_heat, group = packed
        chosen = lax.dynamic_index_in_dim(conduct, group, 0, keepdims=False)
        return solve_point(chosen, point_gradient, point_heat)
    qp_flux = lax.map(one_point, (gradient, heat, sample_choice_per_point))
    residual = jnp.dot(qp_flux, signs.T, precision=HIGHEST) / 4.0
    rows = global_entry_position[element_corner_ids]
    nodal_flux = jnp.zeros((GLOBAL_MESH_PTS,), jnp.float32).at[rows.reshape(-1)].add(residual.reshape(-1))
    return (qp_flux, nodal_flux)
```

```python
import math

import jax
import jax.numpy as jnp
import numpy as np
from jax import lax
from jax.sharding import PartitionSpec as P

PHASES = 3

HIGHEST = lax.Precision.HIGHEST


def mode_tables(width, slab):
    half = width // 2
    mode = np.arange(width)
    number = np.where(mode <= half, mode, mode - half)
    angle = 2.0 * np.pi * (number[:, None] * np.arange(width)[None, :] % width) / width
    basis = np.where((mode <= half)[:, None], np.cos(angle), np.sin(angle)) * math.sqrt(2.0 / width)
    basis[0] /= math.sqrt(2.0)
    basis[half] /= math.sqrt(2.0)
    line = 4.0 * np.sin(np.pi * number / width) ** 2
    plane = line[:, None] + line[None, :]
    rho = 1.0 + plane / 2.0 - np.sqrt(plane + plane * plane / 4.0)
    zero = plane == 0.0
    norm = np.where(zero, 0.0, 1.0 / np.where(zero, 1.0, 1.0 / rho - rho))
    step = rho**slab
    loop = rho**width
    keep = np.where(zero, 0.0, 1.0 - loop)
    scale = np.where(zero, 1.0, 1.0 / np.where(zero, 1.0, 1.0 - loop))
    f32 = lambda table: table.astype(np.float32)
    return f32(basis), f32(rho), f32(norm), f32(step), f32(keep), f32(scale)


def corner_signs():
    table = [
        [2.0 * (corner >> device_axis & 1) - 1.0 for device_axis in range(3)] for corner in range(8)
    ]
    return jnp.array(table, dtype=jnp.float32)


def base_field(voxel_material_ids, fiber_fraction, phase_lookup_table):
    conduct = jnp.zeros(fiber_fraction.shape, jnp.float32)
    for phase in range(PHASES):
        conduct = conduct + jnp.where(voxel_material_ids == phase, phase_lookup_table[phase], 0.0)
    return conduct * fiber_fraction


def spread_tails(tails, step, keep, scale):
    slabs = tails.shape[0]
    right = tails[0, 0]
    left = tails[slabs - 1, 1]
    for i in range(1, slabs):
        right = tails[i, 0] + step * right
        left = tails[slabs - 1 - i, 1] + step * left
    rights, lefts = [right], [left]
    for j in range(slabs - 1):
        rights.append(keep * tails[j, 0] + step * rights[-1])
        lefts.append(keep * tails[slabs - 1 - j, 1] + step * lefts[-1])
    return jnp.stack([jnp.stack([r, l]) for r, l in zip(rights, lefts[::-1])]) * scale


def on_device(
    voxel_material_ids,
    fiber_fraction,
    material_matrix_diffusivity,
    mesh_point_thermal_state,
    element_corner_ids,
    global_entry_position,
    sample_choice_per_point,
):
    macro_index = lax.axis_index("macro")
    pencil_index = lax.axis_index("pencil")
    slab = fiber_fraction.shape[1]
    width = fiber_fraction.shape[3]
    volume = float(width**3)
    slabs = width // slab
    per_device = element_corner_ids.shape[0]
    own_nodes = mesh_point_thermal_state.shape[0]
    basis, rho, norm, step, keep, scale = mode_tables(width, slab)

    packed = jnp.concatenate(
        [
            mesh_point_thermal_state,
            global_entry_position.astype(jnp.float32),
            sample_choice_per_point.astype(jnp.float32),
            element_corner_ids.reshape(-1).astype(jnp.float32),
        ]
    )
    gathered = lax.all_gather(packed, "macro", axis=0, tiled=False)

    conduct = base_field(voxel_material_ids[0], fiber_fraction[0], material_matrix_diffusivity[0])
    total = jnp.sum(conduct)
    total_square = jnp.sum(conduct * conduct)
    modes = jnp.einsum("xyz,bz->xyb", conduct, basis, precision=HIGHEST)
    modes = jnp.einsum("ay,xyb->xab", basis, modes, precision=HIGHEST) * norm
    right = modes[0]
    left = modes[slab - 1]
    for i in range(1, slab):
        right = modes[i] + rho * right
        left = modes[slab - 1 - i] + rho * left
    corner = (jnp.arange(width)[:, None] == 0) & (jnp.arange(width)[None, :] == 0)
    right = jnp.where(corner, total, right)
    left = jnp.where(corner, total_square, left)
    tails = lax.all_to_all(jnp.stack([right, left]), "pencil", 1, 0, tiled=True)
    rows = lambda table: lax.dynamic_slice_in_dim(jnp.asarray(table), pencil_index * slab, slab)
    tails = spread_tails(
        tails.reshape(slabs, 2, slab, width), rows(step), rows(keep), rows(scale)
    )
    tails = lax.all_to_all(tails.reshape(2 * slabs, slab, width), "pencil", 0, 1, tiled=True)
    mean = tails[0, 0, 0] / volume
    mean_square = tails[1, 0, 0] / volume
    before = jnp.where(corner, 0.0, tails[0])
    after = jnp.where(corner, 0.0, tails[1])
    ahead = [before]
    for i in range(slab):
        ahead.append(modes[i] + rho * ahead[-1])
    ahead.append(rho * ahead[-1])
    behind = [after, rho * after]
    for i in range(slab - 1, -1, -1):
        behind.append(rho * (modes[i] + behind[-1]))
    behind = behind[::-1]
    potential = jnp.stack([p + q for p, q in zip(ahead, behind)])
    rise = potential[1:-1] - potential[:-2]
    potential = potential[1:]
    shifted = jnp.asarray(basis.astype(np.float64) - np.roll(basis.astype(np.float64), 1, axis=1), jnp.float32)
    synth = lambda field, y, z: jnp.einsum(
        "ay,xaz->xyz", y, jnp.einsum("xab,bz->xaz", field, z, precision=HIGHEST), precision=HIGHEST
    )
    psi_x = synth(rise, basis, basis)
    psi_y = synth(potential, shifted, basis)
    psi_z = synth(potential, basis, shifted)
    next_y = lambda f: jnp.roll(f, -1, axis=1) - f
    next_z = lambda f: jnp.roll(f, -1, axis=2) - f
    here_y, here_z = psi_y[:-1], psi_z[:-1]
    e_xy, e_yy, e_zy = psi_y[1:] - here_y, next_y(here_y), next_z(here_y)
    e_xz, e_yz, e_zz = psi_z[1:] - here_z, next_y(here_z), next_z(here_z)
    e_yx, e_zx = next_y(psi_x), next_z(psi_x)
    e_xx = mean - conduct - e_yy - e_zz
    e = [[e_xx, e_yx, e_zx], [e_xy, e_yy, e_zy], [e_xz, e_yz, e_zz]]
    plain = [[None] * 3 for _ in range(3)]
    weighted = [[None] * 3 for _ in range(3)]
    for i in range(3):
        for j in range(i, 3):
            product = e[i][0] * e[j][0] + e[i][1] * e[j][1] + e[i][2] * e[j][2]
            plain[i][j] = plain[j][i] = jnp.sum(product) / volume
            weighted[i][j] = weighted[j][i] = jnp.sum(conduct * product) / volume
    plain = jnp.stack([jnp.stack(r) for r in plain])
    weighted = jnp.stack([jnp.stack(r) for r in weighted])

    points = gathered.shape[0]
    temperature = gathered[:, :own_nodes].reshape(-1)
    entry = gathered[:, own_nodes : 2 * own_nodes].reshape(-1)
    assign = gathered[:, 2 * own_nodes]
    corners = gathered[:, 2 * own_nodes + 1 :].reshape(points, 8)
    node_ids = jnp.arange(temperature.shape[0]).astype(jnp.float32)
    picks = corners[:, :, None] == node_ids
    theta = jnp.sum(jnp.where(picks, temperature, 0.0), axis=2)
    rows_of = jnp.sum(jnp.where(picks, entry, 0.0), axis=2)
    signs = corner_signs()
    gradient = jnp.dot(theta, signs, precision=HIGHEST) / 4.0
    heat = jnp.sum(theta, axis=1) / 8.0
    radiative = heat**3
    reference_k = jnp.sqrt(mean_square + 2.0 * radiative * mean + radiative * radiative)
    inverse_k = 1.0 / reference_k
    first = jnp.sum(plain[None] * gradient[:, None, :], axis=2)
    second = jnp.sum(weighted[None] * gradient[:, None, :], axis=2)
    flux = (
        second * (inverse_k * inverse_k)[:, None]
        - first * (inverse_k * (2.0 - radiative * inverse_k))[:, None]
    )
    share = gradient * (mean + radiative)[:, None] / float(slabs)
    here = assign == macro_index.astype(jnp.float32)
    flux = jnp.where(here[:, None], flux + share, 0.0)
    residual = jnp.dot(flux, signs.T, precision=HIGHEST) / 4.0
    nodal = jnp.sum(jnp.where(rows_of[:, :, None] == node_ids, residual[:, :, None], 0.0), axis=(0, 1))
    parts = jnp.concatenate([flux, nodal.reshape(points, own_nodes)], axis=1)
    parts = lax.psum(parts, ("macro", "pencil"))
    mine = lax.dynamic_slice_in_dim(parts, macro_index * per_device, per_device)
    return (mine[:, :3], mine[0, 3:])


def solution(mesh):
    in_specs = (
        P("macro", "pencil", None, None),
        P("macro", "pencil", None, None),
        P("macro", None),
        P("macro"),
        P("macro", None),
        P("macro"),
        P("macro"),
    )
    out_specs = (P("macro", None), P("macro"))
    return jax.shard_map(
        on_device, mesh=mesh, in_specs=in_specs, out_specs=out_specs, check_vma=False
    )
```

```python
import math

import jax
import jax.numpy as jnp
import ml_dtypes
import numpy as np
from jax import lax
from jax.experimental import pallas as pl
from jax.experimental.pallas import tpu as pltpu
from jax.sharding import PartitionSpec as P

PHASES = 3
LANES = 128
ROWS = 8
VMEM_BYTES = 48 * 1024 * 1024

HIGHEST = lax.Precision.HIGHEST


def split_table(table):
    high = table.astype(ml_dtypes.bfloat16)
    low = (table - high.astype(np.float64)).astype(ml_dtypes.bfloat16)
    return high, low


def from_right(table):
    high, low = split_table(table)
    return np.block([[high, low], [high, low]])


def from_left(table):
    high, low = split_table(table)
    return np.block([[high, high], [low, low]])


def mode_tables(width, slab):
    half = width // 2
    mode = np.arange(width)
    number = np.where(mode <= half, mode, mode - half)
    angle = 2.0 * np.pi * (number[:, None] * np.arange(width)[None, :] % width) / width
    basis = np.where((mode <= half)[:, None], np.cos(angle), np.sin(angle)) * math.sqrt(2.0 / width)
    basis[0] /= math.sqrt(2.0)
    basis[half] /= math.sqrt(2.0)
    slope = basis - np.roll(basis, 1, axis=1)
    slope[0] = 0.0
    line = 4.0 * np.sin(np.pi * number / width) ** 2
    plane = line[:, None] + line[None, :]
    rho = 1.0 + plane / 2.0 - np.sqrt(plane + plane * plane / 4.0)
    zero = plane == 0.0
    norm = np.where(zero, 0.0, 1.0 / np.where(zero, 1.0, 1.0 / rho - rho))
    scale = np.where(zero, 1.0, 1.0 / np.where(zero, 1.0, 1.0 - rho**width))
    f32 = lambda table: table.astype(np.float32)
    return dict(
        basis=basis,
        slope=slope,
        rho=f32(rho),
        norm=f32(norm),
        step=f32(rho**slab),
        chip_step=f32(rho ** (2 * slab)),
        scale=f32(scale),
    )


def halves(data):
    high = data.astype(jnp.bfloat16)
    low = (data - high.astype(jnp.float32)).astype(jnp.bfloat16)
    return high, low


def beside(data):
    return jnp.concatenate(halves(data), axis=1)


def stacked(data):
    return jnp.concatenate(halves(data), axis=0)


def product(left, right):
    return jnp.dot(left, right, preferred_element_type=jnp.float32)


def corner_mask(shape):
    row = lax.broadcasted_iota(jnp.int32, shape, 0)
    lane = lax.broadcasted_iota(jnp.int32, shape, 1)
    return (row == 0) & (lane == 0)


def analyse_kernel(
    material_ref, ids_ref, fiber_ref, right_ref, left_ref, norm_ref, rho_ref,
    conduct_ref, modes_ref, keep_ref, give_ref, sums_ref,
):
    slab, width = fiber_ref.shape[1], fiber_ref.shape[3]
    odd = lax.rem(lax.axis_index("pencil"), 2) == 1
    sums_ref[...] = jnp.zeros_like(sums_ref)

    def pair(step, carry):
        planes = []
        for part in range(2):
            x = 2 * step + part
            ids = ids_ref[0, x]
            conduct = jnp.zeros((width, width), jnp.float32)
            for phase in range(PHASES):
                conduct = jnp.where(ids == phase, material_ref[0, phase], conduct)
            conduct = conduct * fiber_ref[0, x]
            conduct_ref[x] = conduct
            tiles = conduct.reshape(width // ROWS, ROWS, width)
            sums_ref[0] += jnp.sum(tiles, axis=0)
            sums_ref[1] += jnp.sum(tiles * tiles, axis=0)
            planes.append(beside(conduct))
        lines = product(jnp.concatenate(planes, axis=0), right_ref[...])
        lines = lines[:, :width] + lines[:, width:]
        lines = jnp.concatenate([lines[:width], lines[width:]], axis=1)
        modes = product(left_ref[...], stacked(lines))
        modes = modes[:width] + modes[width:]
        norm = norm_ref[...]
        modes_ref[2 * step] = modes[:, :width] * norm
        modes_ref[2 * step + 1] = modes[:, width:] * norm
        return carry

    lax.fori_loop(0, slab // 2, pair, 0)
    total = jnp.sum(sums_ref[0])
    total_square = jnp.sum(sums_ref[1])

    def chunk(index, carry):
        at = pl.ds(pl.multiple_of(index * ROWS, ROWS), ROWS)
        rho = rho_ref[at]
        right = modes_ref[0, at]
        left = modes_ref[slab - 1, at]
        for x in range(1, slab):
            right = modes_ref[x, at] + rho * right
            left = modes_ref[slab - 1 - x, at] + rho * left
        corner = corner_mask(right.shape) & (index == 0)
        right = jnp.where(corner, total, right)
        left = jnp.where(corner, total_square, left)
        keep_ref[at] = jnp.where(odd, left, right)
        give_ref[at] = jnp.where(odd, right, left)
        return carry

    lax.fori_loop(0, width // ROWS, chunk, 0)


def moments_kernel(
    conduct_ref, modes_ref, own_ref, other_ref, extra_ref, rho_ref,
    right_basis_ref, right_slope_ref, left_basis_ref, left_slope_ref,
    out_ref, potential_ref, rise_ref, px_ref, py_ref, pz_ref,
):
    slab, width = conduct_ref.shape[0], conduct_ref.shape[2]
    volume = float(width**3)
    pencil = lax.axis_index("pencil")
    odd = lax.rem(pencil, 2) == 1

    def sweep(index, carry):
        at = pl.ds(pl.multiple_of(index * ROWS, ROWS), ROWS)
        rho = rho_ref[at]
        corner = corner_mask(rho.shape) & (index == 0)
        own, other = own_ref[at], other_ref[at]
        before = jnp.where(corner, 0.0, jnp.where(odd, other, own))
        after = jnp.where(corner, 0.0, jnp.where(odd, own, other))
        behind = [after, rho * after]
        for x in range(slab - 1, -1, -1):
            behind.append(rho * (modes_ref[x, at] + behind[-1]))
        behind = behind[::-1]
        ahead = before
        last = ahead + behind[0]
        for x in range(slab + 1):
            ahead = rho * ahead
            if x < slab:
                ahead = ahead + modes_ref[x, at]
            here = ahead + behind[x + 1]
            potential_ref[x, at] = here
            rise_ref[x, at] = here - last
            last = here
        return carry

    lax.fori_loop(0, width // ROWS, sweep, 0)

    def put(ref, x, plane):
        ref[x, :width] = plane
        ref[x, width:] = plane[:ROWS]

    def synthesise(x):
        along = beside(potential_ref[x])
        rise = product(beside(rise_ref[x]), right_basis_ref[...])
        slope = product(along, right_slope_ref[...])
        plain = product(along, right_basis_ref[...])
        rise = rise[:, :width] + rise[:, width:]
        slope = slope[:, :width] + slope[:, width:]
        plain = plain[:, :width] + plain[:, width:]
        both = product(left_basis_ref[...], stacked(jnp.concatenate([slope, rise], axis=1)))
        both = both[:width] + both[width:]
        third = product(left_slope_ref[...], stacked(plain))
        third = third[:width] + third[width:]
        put(pz_ref, x, both[:, :width])
        put(px_ref, x, both[:, width:])
        put(py_ref, x, third)

    corner = corner_mask((ROWS, width))
    own = jnp.sum(jnp.where(corner, own_ref[:ROWS], 0.0))
    other = jnp.sum(jnp.where(corner, other_ref[:ROWS], 0.0))
    first = jnp.where(odd, other, own)
    second = jnp.where(odd, own, other)
    mean = first / volume

    def plane(step, totals):
        x = jnp.maximum(step - 2, 0)
        totals = list(totals)
        for chunk in range(width // ROWS):
            at = pl.ds(chunk * ROWS, ROWS)
            down = pl.ds(chunk * ROWS + 1, ROWS)
            conduct = conduct_ref[x, at]
            px, py, pz = px_ref[x, at], py_ref[x, at], pz_ref[x, at]
            turn = lambda field: pltpu.roll(field, width - 1, 1) - field
            e_yx, e_zx = px_ref[x, down] - px, turn(px)
            e_xy, e_yy, e_zy = py_ref[x + 1, at] - py, py_ref[x, down] - py, turn(py)
            e_xz, e_yz, e_zz = pz_ref[x + 1, at] - pz, pz_ref[x, down] - pz, turn(pz)
            e_xx = (mean - conduct) - (e_yy + e_zz)
            e = ((e_xx, e_yx, e_zx), (e_xy, e_yy, e_zy), (e_xz, e_yz, e_zz))
            at_entry = 0
            for i in range(3):
                for j in range(i, 3):
                    term = e[i][0] * e[j][0] + e[i][1] * e[j][1] + e[i][2] * e[j][2]
                    totals[at_entry] = totals[at_entry] + term
                    totals[6 + at_entry] = totals[6 + at_entry] + conduct * term
                    at_entry += 1
        synthesise(jnp.minimum(step, slab))
        return tuple(jnp.where(step < 2, 0.0, total) for total in totals)

    nothing = jnp.zeros((ROWS, width), jnp.float32)
    totals = lax.fori_loop(0, slab + 2, plane, (nothing,) * 12)
    lines = [jnp.sum(total, axis=0, keepdims=True) for total in totals]
    lines = jnp.concatenate(lines + [jnp.zeros((4, width), jnp.float32)], axis=0)
    column = jnp.sum(lines, axis=1, keepdims=True)
    row = lax.broadcasted_iota(jnp.int32, (16, width), 0)
    lane = lax.broadcasted_iota(jnp.int32, (16, width), 1)
    once = jnp.where(pencil == 0, 1.0, 0.0)
    column = jnp.where(row == 12, first * once, jnp.where(row == 13, second * once, column))
    out_ref[...] = jnp.sum(jnp.where(row == lane, column, 0.0), axis=0, keepdims=True) + extra_ref[...] * once


def close_kernel(nodes_own, volume, table_ref, flux_ref, nodal_ref):
    points = table_ref.shape[0]
    macro = lax.axis_index("macro")
    table = table_ref[...]
    lane = lax.broadcasted_iota(jnp.int32, (points, LANES), 1)
    row = lax.broadcasted_iota(jnp.int32, (points, LANES), 0)
    column = lambda index: table[:, index : index + 1]

    def along_lanes(start):
        spread = jnp.zeros((points, LANES), jnp.float32)
        for node in range(nodes_own):
            spread = jnp.where(lane == row * nodes_own + node, column(start + node), spread)
        return jnp.sum(spread, axis=0, keepdims=True)

    temperature = along_lanes(16)
    entry = along_lanes(16 + nodes_own)
    assign = column(16 + 2 * nodes_own)
    theta, rows = [], []
    for corner in range(8):
        pick = lane.astype(jnp.float32) == column(17 + 2 * nodes_own + corner)
        theta.append(jnp.sum(jnp.where(pick, temperature, 0.0), axis=1, keepdims=True))
        rows.append(jnp.sum(jnp.where(pick, entry, 0.0), axis=1, keepdims=True))
    sign = lambda corner, axis: 2.0 * (corner >> axis & 1) - 1.0
    gradient = [sum(sign(a, d) * theta[a] for a in range(8)) / 4.0 for d in range(3)]
    heat = sum(theta) / 8.0
    chosen = jnp.where(
        lax.broadcasted_iota(jnp.int32, (points, points), 1).astype(jnp.float32) == assign, 1.0, 0.0
    )
    moments = jnp.dot(chosen, table, precision=HIGHEST, preferred_element_type=jnp.float32) / volume
    moment = lambda index: moments[:, index : index + 1]
    mean, mean_square = moment(12), moment(13)
    radiative = heat * heat * heat
    inverse_k = lax.rsqrt(mean_square + 2.0 * radiative * mean + radiative * radiative)
    order = ((0, 1, 2), (1, 3, 4), (2, 4, 5))
    flux = []
    for d in range(3):
        plain = sum(moment(order[d][j]) * gradient[j] for j in range(3))
        weighted = sum(moment(6 + order[d][j]) * gradient[j] for j in range(3))
        flux.append(
            gradient[d] * (mean + radiative)
            + weighted * (inverse_k * inverse_k)
            - plain * (inverse_k * (2.0 - radiative * inverse_k))
        )
    spread = jnp.zeros((points, LANES), jnp.float32)
    for d in range(3):
        spread = jnp.where(lane == d, flux[d], spread)
    mine = jnp.sum(jnp.where(row == macro, spread, 0.0), axis=0, keepdims=True)
    flux_ref[...] = mine[:, :3]
    assembled = jnp.zeros((points, LANES), jnp.float32)
    for corner in range(8):
        residual = sum(sign(corner, d) * flux[d] for d in range(3)) / 4.0
        hit = lane.astype(jnp.float32) == rows[corner] - (macro * nodes_own).astype(jnp.float32)
        assembled = assembled + jnp.where(hit, residual, 0.0)
    nodal_ref[...] = jnp.sum(assembled, axis=0, keepdims=True)[:, :nodes_own]


def on_device(
    voxel_material_ids,
    fiber_fraction,
    material_matrix_diffusivity,
    mesh_point_thermal_state,
    element_corner_ids,
    global_entry_position,
    sample_choice_per_point,
):
    slab = fiber_fraction.shape[1]
    width = fiber_fraction.shape[3]
    volume = float(width**3)
    own_nodes = mesh_point_thermal_state.shape[0]
    pencils = lax.axis_size("pencil")
    chips = pencils // 2
    groups = lax.axis_size("macro")
    tables = mode_tables(width, slab)
    plane = jax.ShapeDtypeStruct((width, width), jnp.float32)
    block = jax.ShapeDtypeStruct((slab, width, width), jnp.float32)
    params = pltpu.CompilerParams(vmem_limit_bytes=VMEM_BYTES)
    vmem = pl.BlockSpec(memory_space=pltpu.VMEM)
    smem = pl.BlockSpec(memory_space=pltpu.SMEM)

    extra = jnp.concatenate(
        [
            mesh_point_thermal_state,
            global_entry_position.astype(jnp.float32),
            sample_choice_per_point.astype(jnp.float32),
            element_corner_ids.reshape(-1).astype(jnp.float32),
        ]
    )
    extra = jnp.pad(extra, (16, LANES - 16 - extra.shape[0])).reshape(1, LANES)

    conduct, modes, keep, give = pl.pallas_call(
        analyse_kernel,
        out_shape=(block, block, plane, plane),
        in_specs=[smem] + [vmem] * 6,
        out_specs=(vmem,) * 4,
        scratch_shapes=[pltpu.VMEM((2, ROWS, width), jnp.float32)],
        compiler_params=params,
        name="analyse",
    )(
        material_matrix_diffusivity,
        voxel_material_ids,
        fiber_fraction,
        from_right(tables["basis"].T),
        from_left(tables["basis"]),
        tables["norm"],
        tables["rho"],
    )

    swap = [(i, i ^ 1) for i in range(pencils)]

    def from_chip(array, away):
        perm = [(i, (i + (2 * away if i % 2 == 0 else -2 * away)) % pencils) for i in range(pencils)]
        return lax.ppermute(array, "pencil", perm)

    step, chip_step, scale = tables["step"], tables["chip_step"], tables["scale"]
    chip = lax.ppermute(give, "pencil", swap) + step * keep
    coming = [from_chip(chip, away) for away in range(1, chips)] + [chip]
    own = coming[-1]
    for tail in coming[-2::-1]:
        own = tail + chip_step * own
    own = own * scale
    corner = corner_mask((width, width))
    other = lax.ppermute(jnp.where(corner, 0.0, keep) + step * own, "pencil", swap)

    field = (slab + 1, width, width)
    padded = (slab + 1, width + ROWS, width)
    moments = pl.pallas_call(
        moments_kernel,
        out_shape=jax.ShapeDtypeStruct((1, LANES), jnp.float32),
        in_specs=[vmem] * 10,
        out_specs=vmem,
        scratch_shapes=[pltpu.VMEM(s, jnp.float32) for s in (field, field, padded, padded, padded)],
        compiler_params=params,
        name="moments",
    )(
        conduct,
        modes,
        own,
        other,
        extra,
        tables["rho"],
        from_right(tables["basis"]),
        from_right(tables["slope"]),
        from_left(tables["basis"].T),
        from_left(tables["slope"].T),
    )

    table = jnp.broadcast_to(moments, (pencils, LANES))
    table = jnp.sum(lax.all_to_all(table, "pencil", 0, 0, tiled=True), axis=0, keepdims=True)
    table = lax.all_to_all(jnp.broadcast_to(table, (groups, LANES)), "macro", 0, 0, tiled=True)
    flux, nodal = pl.pallas_call(
        lambda *refs: close_kernel(own_nodes, volume, *refs),
        out_shape=(
            jax.ShapeDtypeStruct((1, 3), jnp.float32),
            jax.ShapeDtypeStruct((1, own_nodes), jnp.float32),
        ),
        in_specs=[vmem],
        out_specs=(vmem, vmem),
        name="close",
    )(table)
    return (flux, nodal.reshape(own_nodes))


def solution(mesh):
    in_specs = (
        P("macro", "pencil", None, None),
        P("macro", "pencil", None, None),
        P("macro", None),
        P("macro"),
        P("macro", None),
        P("macro"),
        P("macro"),
    )
    out_specs = (P("macro", None), P("macro"))
    return jax.shard_map(
        on_device, mesh=mesh, in_specs=in_specs, out_specs=out_specs, check_vma=False
    )
```

```python
import math

import jax
import jax.numpy as jnp
import ml_dtypes
import numpy as np
from jax import lax
from jax.experimental import pallas as pl
from jax.experimental.pallas import tpu as pltpu
from jax.sharding import PartitionSpec as P

PHASES = 3
LANES = 128
ROWS = 8
PIECES = 4
VMEM_BYTES = 48 * 1024 * 1024
HBM_INPUTS_BYTES = 56 * 1024 * 1024

HIGHEST = lax.Precision.HIGHEST


def split_table(table):
    high = table.astype(ml_dtypes.bfloat16)
    low = (table - high.astype(np.float64)).astype(ml_dtypes.bfloat16)
    return high, low


def from_right(table):
    high, low = split_table(table)
    return np.block([[high, low], [high, low]])


def from_left(table):
    high, low = split_table(table)
    return np.block([[high, high], [low, low]])


def mode_tables(width, slab):
    half = width // 2
    mode = np.arange(width)
    number = np.where(mode <= half, mode, mode - half)
    angle = 2.0 * np.pi * (number[:, None] * np.arange(width)[None, :] % width) / width
    basis = np.where((mode <= half)[:, None], np.cos(angle), np.sin(angle)) * math.sqrt(2.0 / width)
    basis[0] /= math.sqrt(2.0)
    basis[half] /= math.sqrt(2.0)
    slope = basis - np.roll(basis, 1, axis=1)
    slope[0] = 0.0
    line = 4.0 * np.sin(np.pi * number / width) ** 2
    plane = line[:, None] + line[None, :]
    rho = 1.0 + plane / 2.0 - np.sqrt(plane + plane * plane / 4.0)
    zero = plane == 0.0
    norm = np.where(zero, 0.0, 1.0 / np.where(zero, 1.0, 1.0 / rho - rho))
    scale = np.where(zero, 1.0, 1.0 / np.where(zero, 1.0, 1.0 - rho**width))
    f32 = lambda table: table.astype(np.float32)
    return dict(
        basis=basis,
        slope=slope,
        rho=f32(rho),
        norm=f32(norm),
        step=f32(rho**slab),
        chip_step=f32(rho ** (2 * slab)),
        scale=f32(scale),
    )


def halves(data):
    high = data.astype(jnp.bfloat16)
    low = (data - high.astype(jnp.float32)).astype(jnp.bfloat16)
    return high, low


def beside(data):
    return jnp.concatenate(halves(data), axis=1)


def stacked(data):
    return jnp.concatenate(halves(data), axis=0)


def product(left, right):
    return jnp.dot(left, right, preferred_element_type=jnp.float32)


def corner_mask(shape):
    row = lax.broadcasted_iota(jnp.int32, shape, 0)
    lane = lax.broadcasted_iota(jnp.int32, shape, 1)
    return (row == 0) & (lane == 0)


def analyse_kernel(
    material_hbm, ids_hbm, fiber_hbm, right_hbm, left_hbm, norm_hbm, rho_hbm,
    conduct_hbm, modes_hbm, keep_ref, give_ref,
    conduct_ref, modes_ref, sums_ref, material_ref, ids_ref, fiber_ref, right_ref, left_ref, norm_ref, rho_ref,
    table_sems, ids_sems, fiber_sems, conduct_sems, modes_sems,
):
    slab, width = fiber_ref.shape[0], fiber_ref.shape[2]
    group = slab // PIECES
    odd = lax.rem(lax.axis_index("pencil"), 2) == 1

    def ids_copy(piece):
        at = pl.ds(piece * group, group)
        return pltpu.make_async_copy(ids_hbm.at[0, at], ids_ref.at[at], ids_sems.at[piece])

    def fiber_copy(piece):
        at = pl.ds(piece * group, group)
        return pltpu.make_async_copy(fiber_hbm.at[0, at], fiber_ref.at[at], fiber_sems.at[piece])

    def conduct_copy(piece):
        at = pl.ds(piece * group, group)
        return pltpu.make_async_copy(conduct_ref.at[at], conduct_hbm.at[at], conduct_sems.at[piece])

    def modes_copy(piece):
        at = pl.ds(piece * group, group)
        return pltpu.make_async_copy(modes_ref.at[at], modes_hbm.at[at], modes_sems.at[piece])

    tables = [
        pltpu.make_async_copy(source, target, table_sems.at[index])
        for index, (source, target) in enumerate(
            (
                (material_hbm, material_ref),
                (right_hbm, right_ref),
                (left_hbm, left_ref),
                (norm_hbm, norm_ref),
                (rho_hbm, rho_ref),
            )
        )
    ]
    tables[0].start()
    ids_copy(0).start()
    fiber_copy(0).start()
    for copy in tables[1:]:
        copy.start()
    for piece in range(1, PIECES):
        ids_copy(piece).start()
        fiber_copy(piece).start()
    sums_ref[...] = jnp.zeros_like(sums_ref)
    for copy in tables:
        copy.wait()

    def few(piece, carry):
        ids_copy(piece).wait()
        fiber_copy(piece).wait()
        planes = []
        for part in range(group):
            x = group * piece + part
            ids = ids_ref[x]
            conduct = jnp.where(
                ids == 0, material_ref[0, 0], jnp.where(ids == 1, material_ref[0, 1], material_ref[0, 2])
            )
            conduct = conduct * fiber_ref[x]
            conduct_ref[x] = conduct
            tiles = conduct.reshape(width // ROWS, ROWS, width)
            sums_ref[0] += jnp.sum(tiles, axis=0)
            sums_ref[1] += jnp.sum(tiles * tiles, axis=0)
            planes.append(beside(conduct))
        conduct_copy(piece).start()
        lines = product(jnp.concatenate(planes, axis=0), right_ref[...])
        lines = lines[:, :width] + lines[:, width:]
        norm = norm_ref[...]
        for part in range(0, group, 2):
            pair = jnp.concatenate(
                [lines[part * width : (part + 1) * width], lines[(part + 1) * width : (part + 2) * width]], axis=1
            )
            modes = product(left_ref[...], stacked(pair))
            modes = modes[:width] + modes[width:]
            modes_ref[group * piece + part] = modes[:, :width] * norm
            modes_ref[group * piece + part + 1] = modes[:, width:] * norm
        modes_copy(piece).start()
        return carry

    lax.fori_loop(0, PIECES, few, 0)
    total = jnp.sum(sums_ref[0])
    total_square = jnp.sum(sums_ref[1])
    rho = rho_ref[...]
    right = modes_ref[0]
    left = modes_ref[slab - 1]
    for x in range(1, slab):
        right = modes_ref[x] + rho * right
        left = modes_ref[slab - 1 - x] + rho * left
    corner = corner_mask(right.shape)
    right = jnp.where(corner, total, right)
    left = jnp.where(corner, total_square, left)
    keep_ref[...] = jnp.where(odd, left, right)
    give_ref[...] = jnp.where(odd, right, left)
    for piece in range(PIECES):
        conduct_copy(piece).wait()
        modes_copy(piece).wait()


def moments_kernel(
    conduct_ref, modes_ref, own_ref, other_ref, extra_ref, rho_ref,
    right_basis_ref, right_slope_ref, left_basis_ref, left_slope_ref,
    out_ref, potential_ref, rise_ref, px_ref, py_ref, pz_ref, lines_ref,
):
    slab, width = conduct_ref.shape[0], conduct_ref.shape[2]
    volume = float(width**3)
    pencil = lax.axis_index("pencil")
    odd = lax.rem(pencil, 2) == 1

    corner = corner_mask((width, width))
    first_plane = jnp.where(odd, other_ref[...], own_ref[...])
    second_plane = jnp.where(odd, own_ref[...], other_ref[...])
    first = jnp.sum(jnp.where(corner, first_plane, 0.0)[:ROWS])
    second = jnp.sum(jnp.where(corner, second_plane, 0.0)[:ROWS])
    mean = first / volume
    rho = rho_ref[...]
    behind = jnp.where(corner, 0.0, second_plane)
    potential_ref[slab] = behind
    behind = rho * behind
    potential_ref[slab - 1] = behind
    for x in range(slab - 2, -1, -1):
        behind = rho * (modes_ref[x + 1] + behind)
        potential_ref[x] = behind
    ahead = jnp.where(corner, 0.0, first_plane)
    last = ahead + rho * (modes_ref[0] + behind)
    for x in range(slab + 1):
        ahead = rho * ahead
        if x < slab:
            ahead = ahead + modes_ref[x]
        here = ahead + potential_ref[x]
        potential_ref[x] = here
        rise_ref[x] = here - last
        last = here

    def put(ref, x, plane):
        ref[x, :width] = plane
        ref[x, width:] = plane[:ROWS]

    def along_z(x):
        along = beside(potential_ref[x])
        rise = product(beside(rise_ref[x]), right_basis_ref[...])
        slope = product(along, right_slope_ref[...])
        plain = product(along, right_basis_ref[...])
        for place, lines in enumerate((slope, rise, plain)):
            high, low = halves(lines[:, :width] + lines[:, width:])
            lanes = pl.ds(place * width, width)
            lines_ref[:width, lanes] = high
            lines_ref[width:, lanes] = low

    def along_y(x):
        both = product(left_basis_ref[...], lines_ref[:, : 2 * width])
        both = both[:width] + both[width:]
        third = product(left_slope_ref[...], lines_ref[:, 2 * width :])
        third = third[:width] + third[width:]
        put(pz_ref, x, both[:, :width])
        put(px_ref, x, both[:, width:])
        put(py_ref, x, third)

    def plane(step, totals):
        x = jnp.maximum(step - 3, 0)
        totals = list(totals)
        for chunk in range(width // ROWS):
            at = pl.ds(chunk * ROWS, ROWS)
            down = pl.ds(chunk * ROWS + 1, ROWS)
            conduct = conduct_ref[x, at]
            px, py, pz = px_ref[x, at], py_ref[x, at], pz_ref[x, at]
            turn = lambda field: pltpu.roll(field, width - 1, 1) - field
            e_yx, e_zx = px_ref[x, down] - px, turn(px)
            e_xy, e_yy, e_zy = py_ref[x + 1, at] - py, py_ref[x, down] - py, turn(py)
            e_xz, e_yz, e_zz = pz_ref[x + 1, at] - pz, pz_ref[x, down] - pz, turn(pz)
            e_xx = (mean - conduct) - (e_yy + e_zz)
            e = ((e_xx, e_yx, e_zx), (e_xy, e_yy, e_zy), (e_xz, e_yz, e_zz))
            at_entry = 0
            for i in range(3):
                for j in range(i, 3):
                    term = e[i][0] * e[j][0] + e[i][1] * e[j][1] + e[i][2] * e[j][2]
                    totals[at_entry] = totals[at_entry] + term
                    totals[6 + at_entry] = totals[6 + at_entry] + conduct * term
                    at_entry += 1
        along_y(jnp.clip(step - 1, 0, slab))
        along_z(jnp.minimum(step, slab))
        return tuple(jnp.where(step < 3, 0.0, total) for total in totals)

    nothing = jnp.zeros((ROWS, width), jnp.float32)
    totals = lax.fori_loop(0, slab + 3, plane, (nothing,) * 12)
    lines = [jnp.sum(total, axis=0, keepdims=True) for total in totals]
    lines = jnp.concatenate(lines + [jnp.zeros((4, width), jnp.float32)], axis=0)
    column = jnp.sum(lines, axis=1, keepdims=True)
    row = lax.broadcasted_iota(jnp.int32, (16, width), 0)
    lane = lax.broadcasted_iota(jnp.int32, (16, width), 1)
    once = jnp.where(pencil == 0, 1.0, 0.0)
    column = jnp.where(row == 12, first * once, jnp.where(row == 13, second * once, column))
    out_ref[...] = jnp.sum(jnp.where(row == lane, column, 0.0), axis=0, keepdims=True) + extra_ref[...] * once


def close_kernel(nodes_own, volume, table_ref, flux_ref, nodal_ref):
    points = table_ref.shape[0]
    macro = lax.axis_index("macro")
    table = table_ref[...]
    lane = lax.broadcasted_iota(jnp.int32, (points, LANES), 1)
    row = lax.broadcasted_iota(jnp.int32, (points, LANES), 0)
    column = lambda index: table[:, index : index + 1]

    temperature = jnp.zeros((points, LANES), jnp.float32)
    node_of = jnp.zeros((points, LANES), jnp.float32)
    mine = (macro * nodes_own + lane).astype(jnp.float32)
    for node in range(nodes_own):
        at = row * nodes_own + node
        temperature = jnp.where(lane == at, column(16 + node), temperature)
        node_of = jnp.where(column(16 + nodes_own + node) == mine, at.astype(jnp.float32), node_of)
    temperature = jnp.sum(temperature, axis=0, keepdims=True)
    node_of = jnp.sum(node_of, axis=0, keepdims=True)
    node_of = jnp.where(lane[:1] < nodes_own, node_of, -1.0)
    assign = column(16 + 2 * nodes_own)
    corners = [column(17 + 2 * nodes_own + corner) for corner in range(8)]
    theta = []
    for corner in range(8):
        pick = lane.astype(jnp.float32) == corners[corner]
        theta.append(jnp.sum(jnp.where(pick, temperature, 0.0), axis=1, keepdims=True))
    sign = lambda corner, axis: 2.0 * (corner >> axis & 1) - 1.0
    gradient = [sum(sign(a, d) * theta[a] for a in range(8)) / 4.0 for d in range(3)]
    heat = sum(theta) / 8.0
    chosen = jnp.where(
        lax.broadcasted_iota(jnp.int32, (points, points), 1).astype(jnp.float32) == assign, 1.0, 0.0
    )
    moments = jnp.dot(chosen, table, precision=HIGHEST, preferred_element_type=jnp.float32) / volume
    moment = lambda index: moments[:, index : index + 1]
    mean, mean_square = moment(12), moment(13)
    radiative = heat * heat * heat
    inverse_k = lax.rsqrt(mean_square + 2.0 * radiative * mean + radiative * radiative)
    order = ((0, 1, 2), (1, 3, 4), (2, 4, 5))
    flux = []
    for d in range(3):
        plain = sum(moment(order[d][j]) * gradient[j] for j in range(3))
        weighted = sum(moment(6 + order[d][j]) * gradient[j] for j in range(3))
        flux.append(
            gradient[d] * (mean + radiative)
            + weighted * (inverse_k * inverse_k)
            - plain * (inverse_k * (2.0 - radiative * inverse_k))
        )
    spread = jnp.zeros((points, LANES), jnp.float32)
    for d in range(3):
        spread = jnp.where(lane == d, flux[d], spread)
    flux_ref[...] = jnp.sum(jnp.where(row == macro, spread, 0.0), axis=0, keepdims=True)[:, :3]
    assembled = jnp.zeros((points, LANES), jnp.float32)
    for corner in range(8):
        residual = sum(sign(corner, d) * flux[d] for d in range(3)) / 4.0
        assembled = assembled + jnp.where(corners[corner] == node_of, residual, 0.0)
    nodal_ref[...] = jnp.sum(assembled, axis=0, keepdims=True)[:, :nodes_own]


def on_device(
    voxel_material_ids,
    fiber_fraction,
    material_matrix_diffusivity,
    mesh_point_thermal_state,
    element_corner_ids,
    global_entry_position,
    sample_choice_per_point,
):
    slab = fiber_fraction.shape[1]
    width = fiber_fraction.shape[3]
    volume = float(width**3)
    own_nodes = mesh_point_thermal_state.shape[0]
    pencils = lax.axis_size("pencil")
    chips = pencils // 2
    groups = lax.axis_size("macro")
    tables = mode_tables(width, slab)
    plane = jax.ShapeDtypeStruct((width, width), jnp.float32)
    block = jax.ShapeDtypeStruct((slab, width, width), jnp.float32)
    params = pltpu.CompilerParams(vmem_limit_bytes=VMEM_BYTES)
    vmem = pl.BlockSpec(memory_space=pltpu.VMEM)
    hbm = pl.BlockSpec(memory_space=pltpu.HBM)

    conduct, modes, keep, give = pl.pallas_call(
        analyse_kernel,
        out_shape=(block, block, plane, plane),
        in_specs=[hbm] * 7,
        out_specs=(hbm, hbm, vmem, vmem),
        scratch_shapes=[
            pltpu.VMEM((slab, width, width), jnp.float32),
            pltpu.VMEM((slab, width, width), jnp.float32),
            pltpu.VMEM((2, ROWS, width), jnp.float32),
            pltpu.SMEM((1, PHASES), jnp.float32),
            pltpu.VMEM((slab, width, width), jnp.int32),
            pltpu.VMEM((slab, width, width), jnp.float32),
            pltpu.VMEM((2 * width, 2 * width), jnp.bfloat16),
            pltpu.VMEM((2 * width, 2 * width), jnp.bfloat16),
            pltpu.VMEM((width, width), jnp.float32),
            pltpu.VMEM((width, width), jnp.float32),
            pltpu.SemaphoreType.DMA((5,)),
            pltpu.SemaphoreType.DMA((PIECES,)),
            pltpu.SemaphoreType.DMA((PIECES,)),
            pltpu.SemaphoreType.DMA((PIECES,)),
            pltpu.SemaphoreType.DMA((PIECES,)),
        ],
        compiler_params=pltpu.CompilerParams(vmem_limit_bytes=HBM_INPUTS_BYTES),
        name="analyse",
    )(
        material_matrix_diffusivity,
        voxel_material_ids,
        fiber_fraction,
        from_right(tables["basis"].T),
        from_left(tables["basis"]),
        tables["norm"],
        tables["rho"],
    )

    swap = [(i, i ^ 1) for i in range(pencils)]

    def from_chip(array, away):
        perm = [(i, (i + (2 * away if i % 2 == 0 else -2 * away)) % pencils) for i in range(pencils)]
        return lax.ppermute(array, "pencil", perm)

    step, chip_step, scale = tables["step"], tables["chip_step"], tables["scale"]
    chip = lax.ppermute(give, "pencil", swap) + step * keep
    chip, temperature, entry, assign, corners = lax.optimization_barrier(
        (chip, mesh_point_thermal_state, global_entry_position, sample_choice_per_point, element_corner_ids)
    )
    extra = jnp.concatenate(
        [
            temperature,
            entry.astype(jnp.float32),
            assign.astype(jnp.float32),
            corners.reshape(-1).astype(jnp.float32),
        ]
    )
    extra = jnp.pad(extra, (16, LANES - 16 - extra.shape[0])).reshape(1, LANES)
    coming = [from_chip(chip, away) for away in range(1, chips)] + [chip]
    own = coming[-1]
    for tail in coming[-2::-1]:
        own = tail + chip_step * own
    own = own * scale
    corner = corner_mask((width, width))
    other = lax.ppermute(jnp.where(corner, 0.0, keep) + step * own, "pencil", swap)

    field = (slab + 1, width, width)
    padded = (slab + 1, width + ROWS, width)
    moments = pl.pallas_call(
        moments_kernel,
        out_shape=jax.ShapeDtypeStruct((1, LANES), jnp.float32),
        in_specs=[vmem] * 10,
        out_specs=vmem,
        scratch_shapes=[pltpu.VMEM(s, jnp.float32) for s in (field, field, padded, padded, padded)]
        + [pltpu.VMEM((2 * width, 3 * width), jnp.bfloat16)],
        compiler_params=params,
        name="moments",
    )(
        conduct,
        modes,
        own,
        other,
        extra,
        tables["rho"],
        from_right(tables["basis"]),
        from_right(tables["slope"]),
        from_left(tables["basis"].T),
        from_left(tables["slope"].T),
    )

    table = jnp.broadcast_to(moments, (pencils, LANES))
    table = jnp.sum(lax.all_to_all(table, "pencil", 0, 0, tiled=True), axis=0, keepdims=True)
    table = lax.all_to_all(jnp.broadcast_to(table, (groups, LANES)), "macro", 0, 0, tiled=True)
    flux, nodal = pl.pallas_call(
        lambda *refs: close_kernel(own_nodes, volume, *refs),
        out_shape=(
            jax.ShapeDtypeStruct((1, 3), jnp.float32),
            jax.ShapeDtypeStruct((1, own_nodes), jnp.float32),
        ),
        in_specs=[vmem],
        out_specs=(vmem, vmem),
        name="close",
    )(table)
    return (flux, nodal.reshape(own_nodes))


def solution(mesh):
    in_specs = (
        P("macro", "pencil", None, None),
        P("macro", "pencil", None, None),
        P("macro", None),
        P("macro"),
        P("macro", None),
        P("macro"),
        P("macro"),
    )
    out_specs = (P("macro", None), P("macro"))
    return jax.shard_map(
        on_device, mesh=mesh, in_specs=in_specs, out_specs=out_specs, check_vma=False
    )
```

```python
import math

import jax
import jax.numpy as jnp
import ml_dtypes
import numpy as np
from jax import lax
from jax.experimental import pallas as pl
from jax.experimental.pallas import tpu as pltpu
from jax.sharding import PartitionSpec as P

PHASES = 3
LANES = 128
ROWS = 8
PIECES = 4
VMEM_BYTES = 48 * 1024 * 1024
HBM_INPUTS_BYTES = 56 * 1024 * 1024

HIGHEST = lax.Precision.HIGHEST


def split_table(table):
    high = table.astype(ml_dtypes.bfloat16)
    low = (table - high.astype(np.float64)).astype(ml_dtypes.bfloat16)
    return high, low


def from_right(table):
    high, low = split_table(table)
    return np.block([[high, low], [high, low]])


def from_left(table):
    high, low = split_table(table)
    return np.block([[high, high], [low, low]])


def mode_tables(width, slab):
    half = width // 2
    mode = np.arange(width)
    number = np.where(mode <= half, mode, mode - half)
    angle = 2.0 * np.pi * (number[:, None] * np.arange(width)[None, :] % width) / width
    basis = np.where((mode <= half)[:, None], np.cos(angle), np.sin(angle)) * math.sqrt(2.0 / width)
    basis[0] /= math.sqrt(2.0)
    basis[half] /= math.sqrt(2.0)
    slope = basis - np.roll(basis, 1, axis=1)
    slope[0] = 0.0
    line = 4.0 * np.sin(np.pi * number / width) ** 2
    plane = line[:, None] + line[None, :]
    rho = 1.0 + plane / 2.0 - np.sqrt(plane + plane * plane / 4.0)
    zero = plane == 0.0
    norm = np.where(zero, 0.0, 1.0 / np.where(zero, 1.0, 1.0 / rho - rho))
    scale = np.where(zero, 1.0, 1.0 / np.where(zero, 1.0, 1.0 - rho**width))
    f32 = lambda table: table.astype(np.float32)
    return dict(
        basis=basis,
        slope=slope,
        rho=f32(rho),
        norm=f32(norm),
        step=f32(rho**slab),
        chip_step=f32(rho ** (2 * slab)),
        scale=f32(scale),
    )


def halves(data):
    high = data.astype(jnp.bfloat16)
    low = (data - high.astype(jnp.float32)).astype(jnp.bfloat16)
    return high, low


def beside(data):
    return jnp.concatenate(halves(data), axis=1)


def stacked(data):
    return jnp.concatenate(halves(data), axis=0)


def product(left, right):
    return jnp.dot(left, right, preferred_element_type=jnp.float32)


def corner_mask(shape):
    row = lax.broadcasted_iota(jnp.int32, shape, 0)
    lane = lax.broadcasted_iota(jnp.int32, shape, 1)
    return (row == 0) & (lane == 0)


def analyse_kernel(
    material_hbm, ids_hbm, fiber_hbm, right_hbm, left_hbm, norm_hbm, rho_hbm,
    conduct_hbm, modes_hbm, keep_ref, give_ref,
    conduct_ref, modes_ref, sums_ref, material_ref, ids_ref, fiber_ref, right_ref, left_ref, norm_ref, rho_ref,
    table_sems, ids_sems, fiber_sems, conduct_sems, modes_sems,
):
    slab, width = fiber_ref.shape[0], fiber_ref.shape[2]
    group = slab // PIECES
    odd = lax.rem(lax.axis_index("pencil"), 2) == 1

    def ids_copy(piece):
        at = pl.ds(piece * group, group)
        return pltpu.make_async_copy(ids_hbm.at[0, at], ids_ref.at[at], ids_sems.at[piece])

    def fiber_copy(piece):
        at = pl.ds(piece * group, group)
        return pltpu.make_async_copy(fiber_hbm.at[0, at], fiber_ref.at[at], fiber_sems.at[piece])

    def conduct_copy(piece):
        at = pl.ds(piece * group, group)
        return pltpu.make_async_copy(conduct_ref.at[at], conduct_hbm.at[at], conduct_sems.at[piece])

    def modes_copy(piece):
        at = pl.ds(piece * group, group)
        return pltpu.make_async_copy(modes_ref.at[at], modes_hbm.at[at], modes_sems.at[piece])

    tables = [
        pltpu.make_async_copy(source, target, table_sems.at[index])
        for index, (source, target) in enumerate(
            (
                (material_hbm, material_ref),
                (right_hbm, right_ref),
                (left_hbm, left_ref),
                (norm_hbm, norm_ref),
                (rho_hbm, rho_ref),
            )
        )
    ]
    tables[0].start()
    ids_copy(0).start()
    fiber_copy(0).start()
    for copy in tables[1:]:
        copy.start()
    for piece in range(1, PIECES):
        ids_copy(piece).start()
        fiber_copy(piece).start()
    sums_ref[...] = jnp.zeros_like(sums_ref)
    for copy in tables:
        copy.wait()

    def along_z(piece):
        ids_copy(piece).wait()
        fiber_copy(piece).wait()
        planes = []
        for part in range(group):
            x = group * piece + part
            ids = ids_ref[x]
            conduct = jnp.where(
                ids == 0, material_ref[0, 0], jnp.where(ids == 1, material_ref[0, 1], material_ref[0, 2])
            )
            conduct = conduct * fiber_ref[x]
            conduct_ref[x] = conduct
            tiles = conduct.reshape(width // ROWS, ROWS, width)
            sums_ref[0] += jnp.sum(tiles, axis=0)
            sums_ref[1] += jnp.sum(tiles * tiles, axis=0)
            planes.append(beside(conduct))
        conduct_copy(piece).start()
        lines = product(jnp.concatenate(planes, axis=0), right_ref[...])
        return lines[:, :width] + lines[:, width:]

    def along_y(piece, lines):
        for part in range(0, group, 2):
            pair = jnp.concatenate(
                [lines[part * width : (part + 1) * width], lines[(part + 1) * width : (part + 2) * width]], axis=1
            )
            modes = product(left_ref[...], stacked(pair))
            modes = modes[:width] + modes[width:]
            modes_ref[group * piece + part] = modes[:, :width]
            modes_ref[group * piece + part + 1] = modes[:, width:]
        modes_copy(piece).start()

    lines = along_z(0)
    for piece in range(1, PIECES):
        ahead = along_z(piece)
        along_y(piece - 1, lines)
        lines = ahead
    along_y(PIECES - 1, lines)
    total = jnp.sum(sums_ref[0])
    total_square = jnp.sum(sums_ref[1])
    rho = rho_ref[...]
    right = modes_ref[0]
    left = modes_ref[slab - 1]
    for x in range(1, slab):
        right = modes_ref[x] + rho * right
        left = modes_ref[slab - 1 - x] + rho * left
    corner = corner_mask(right.shape)
    norm = norm_ref[...]
    right = jnp.where(corner, total, right * norm)
    left = jnp.where(corner, total_square, left * norm)
    keep_ref[...] = jnp.where(odd, left, right)
    give_ref[...] = jnp.where(odd, right, left)
    for piece in range(PIECES):
        conduct_copy(piece).wait()
        modes_copy(piece).wait()


def moments_kernel(
    conduct_ref, modes_ref, own_ref, other_ref, extra_ref, rho_ref,
    right_basis_ref, right_slope_ref, left_basis_ref, left_slope_ref,
    out_ref, potential_ref, rise_ref, px_ref, py_ref, pz_ref, lines_ref,
):
    slab, width = conduct_ref.shape[0], conduct_ref.shape[2]
    volume = float(width**3)
    pencil = lax.axis_index("pencil")
    odd = lax.rem(pencil, 2) == 1

    corner = corner_mask((width, width))
    first_plane = jnp.where(odd, other_ref[...], own_ref[...])
    second_plane = jnp.where(odd, own_ref[...], other_ref[...])
    first = jnp.sum(jnp.where(corner, first_plane, 0.0)[:ROWS])
    second = jnp.sum(jnp.where(corner, second_plane, 0.0)[:ROWS])
    mean = first / volume
    rho = rho_ref[...]
    behind = jnp.where(corner, 0.0, second_plane)
    potential_ref[slab] = behind
    behind = rho * behind
    potential_ref[slab - 1] = behind
    for x in range(slab - 2, -1, -1):
        behind = rho * (modes_ref[x + 1] + behind)
        potential_ref[x] = behind
    ahead = jnp.where(corner, 0.0, first_plane)
    last = ahead + rho * (modes_ref[0] + behind)
    for x in range(slab + 1):
        ahead = rho * ahead
        if x < slab:
            ahead = ahead + modes_ref[x]
        here = ahead + potential_ref[x]
        potential_ref[x] = here
        rise_ref[x] = here - last
        last = here
    potential_ref[slab + 1] = last
    rise_ref[slab + 1] = last

    def put(ref, x, plane):
        ref[x, :width] = plane
        ref[x, width:] = plane[:ROWS]

    def along_z(pair):
        planes = [2 * pair, 2 * pair + 1]
        along = jnp.concatenate([beside(potential_ref[x]) for x in planes], axis=0)
        rise = product(jnp.concatenate([beside(rise_ref[x]) for x in planes], axis=0), right_basis_ref[...])
        slope = product(along, right_slope_ref[...])
        plain = product(along, right_basis_ref[...])
        for place, lines in enumerate((slope, rise, plain)):
            high, low = halves(lines[:, :width] + lines[:, width:])
            for part in range(2):
                rows = slice(part * width, (part + 1) * width)
                lanes = pl.ds((2 * part + place if place < 2 else 4 + part) * width, width)
                lines_ref[:width, lanes] = high[rows]
                lines_ref[width:, lanes] = low[rows]

    def along_y(pair):
        third = product(left_slope_ref[...], lines_ref[:, 4 * width :])
        third = third[:width] + third[width:]
        for part in range(2):
            both = product(left_basis_ref[...], lines_ref[:, 2 * part * width : 2 * (part + 1) * width])
            both = both[:width] + both[width:]
            put(pz_ref, 2 * pair + part, both[:, :width])
            put(px_ref, 2 * pair + part, both[:, width:])
            put(py_ref, 2 * pair + part, third[:, part * width : (part + 1) * width])

    pairs = slab // 2 + 1

    def warm(step, carry):
        along_y(jnp.maximum(step - 1, 0))
        along_z(step)
        return carry

    def plane(step, totals):
        totals = list(totals)
        for place in range(2 * (width // ROWS)):
            x = 2 * (step - 3) + place // (width // ROWS)
            chunk = place % (width // ROWS)
            at = pl.ds(chunk * ROWS, ROWS)
            down = pl.ds(chunk * ROWS + 1, ROWS)
            conduct = conduct_ref[x, at]
            px, py, pz = px_ref[x, at], py_ref[x, at], pz_ref[x, at]
            turn = lambda field: pltpu.roll(field, width - 1, 1) - field
            e_yx, e_zx = px_ref[x, down] - px, turn(px)
            e_xy, e_yy, e_zy = py_ref[x + 1, at] - py, py_ref[x, down] - py, turn(py)
            e_xz, e_yz, e_zz = pz_ref[x + 1, at] - pz, pz_ref[x, down] - pz, turn(pz)
            e_xx = (mean - conduct) - (e_yy + e_zz)
            e = ((e_xx, e_yx, e_zx), (e_xy, e_yy, e_zy), (e_xz, e_yz, e_zz))
            at_entry = 0
            for i in range(3):
                for j in range(i, 3):
                    term = e[i][0] * e[j][0] + e[i][1] * e[j][1] + e[i][2] * e[j][2]
                    totals[at_entry] = totals[at_entry] + term
                    totals[6 + at_entry] = totals[6 + at_entry] + conduct * term
                    at_entry += 1
        along_y(jnp.minimum(step - 1, pairs - 1))
        along_z(jnp.minimum(step, pairs - 1))
        return tuple(totals)

    nothing = jnp.zeros((ROWS, width), jnp.float32)
    lax.fori_loop(0, 3, warm, 0)
    totals = lax.fori_loop(3, pairs + 2, plane, (nothing,) * 12)
    lines = [jnp.sum(total, axis=0, keepdims=True) for total in totals]
    lines = jnp.concatenate(lines + [jnp.zeros((4, width), jnp.float32)], axis=0)
    column = jnp.sum(lines, axis=1, keepdims=True)
    row = lax.broadcasted_iota(jnp.int32, (16, width), 0)
    lane = lax.broadcasted_iota(jnp.int32, (16, width), 1)
    once = jnp.where(pencil == 0, 1.0, 0.0)
    column = jnp.where(row == 12, first * once, jnp.where(row == 13, second * once, column))
    out_ref[...] = jnp.sum(jnp.where(row == lane, column, 0.0), axis=0, keepdims=True) + extra_ref[...] * once


def close_kernel(nodes_own, volume, table_ref, flux_ref, nodal_ref):
    points = table_ref.shape[0]
    macro = lax.axis_index("macro")
    table = table_ref[...]
    lane = lax.broadcasted_iota(jnp.int32, (points, LANES), 1)
    row = lax.broadcasted_iota(jnp.int32, (points, LANES), 0)
    column = lambda index: table[:, index : index + 1]

    temperature = jnp.zeros((points, LANES), jnp.float32)
    node_of = jnp.zeros((points, LANES), jnp.float32)
    mine = (macro * nodes_own + lane).astype(jnp.float32)
    for node in range(nodes_own):
        at = row * nodes_own + node
        temperature = jnp.where(lane == at, column(16 + node), temperature)
        node_of = jnp.where(column(16 + nodes_own + node) == mine, at.astype(jnp.float32), node_of)
    temperature = jnp.sum(temperature, axis=0, keepdims=True)
    node_of = jnp.sum(node_of, axis=0, keepdims=True)
    node_of = jnp.where(lane[:1] < nodes_own, node_of, -1.0)
    assign = column(16 + 2 * nodes_own)
    corners = [column(17 + 2 * nodes_own + corner) for corner in range(8)]
    theta = []
    for corner in range(8):
        pick = lane.astype(jnp.float32) == corners[corner]
        theta.append(jnp.sum(jnp.where(pick, temperature, 0.0), axis=1, keepdims=True))
    sign = lambda corner, axis: 2.0 * (corner >> axis & 1) - 1.0
    gradient = [sum(sign(a, d) * theta[a] for a in range(8)) / 4.0 for d in range(3)]
    heat = sum(theta) / 8.0
    chosen = jnp.where(
        lax.broadcasted_iota(jnp.int32, (points, points), 1).astype(jnp.float32) == assign, 1.0, 0.0
    )
    moments = jnp.dot(chosen, table, precision=HIGHEST, preferred_element_type=jnp.float32) / volume
    moment = lambda index: moments[:, index : index + 1]
    mean, mean_square = moment(12), moment(13)
    radiative = heat * heat * heat
    inverse_k = lax.rsqrt(mean_square + 2.0 * radiative * mean + radiative * radiative)
    order = ((0, 1, 2), (1, 3, 4), (2, 4, 5))
    flux = []
    for d in range(3):
        plain = sum(moment(order[d][j]) * gradient[j] for j in range(3))
        weighted = sum(moment(6 + order[d][j]) * gradient[j] for j in range(3))
        flux.append(
            gradient[d] * (mean + radiative)
            + weighted * (inverse_k * inverse_k)
            - plain * (inverse_k * (2.0 - radiative * inverse_k))
        )
    spread = jnp.zeros((points, LANES), jnp.float32)
    for d in range(3):
        spread = jnp.where(lane == d, flux[d], spread)
    flux_ref[...] = jnp.sum(jnp.where(row == macro, spread, 0.0), axis=0, keepdims=True)[:, :3]
    assembled = jnp.zeros((points, LANES), jnp.float32)
    for corner in range(8):
        residual = sum(sign(corner, d) * flux[d] for d in range(3)) / 4.0
        assembled = assembled + jnp.where(corners[corner] == node_of, residual, 0.0)
    nodal_ref[...] = jnp.sum(assembled, axis=0, keepdims=True)[:, :nodes_own]


def on_device(
    voxel_material_ids,
    fiber_fraction,
    material_matrix_diffusivity,
    mesh_point_thermal_state,
    element_corner_ids,
    global_entry_position,
    sample_choice_per_point,
):
    slab = fiber_fraction.shape[1]
    width = fiber_fraction.shape[3]
    volume = float(width**3)
    own_nodes = mesh_point_thermal_state.shape[0]
    pencils = lax.axis_size("pencil")
    chips = pencils // 2
    groups = lax.axis_size("macro")
    tables = mode_tables(width, slab)
    plane = jax.ShapeDtypeStruct((width, width), jnp.float32)
    block = jax.ShapeDtypeStruct((slab, width, width), jnp.float32)
    params = pltpu.CompilerParams(vmem_limit_bytes=VMEM_BYTES)
    vmem = pl.BlockSpec(memory_space=pltpu.VMEM)
    hbm = pl.BlockSpec(memory_space=pltpu.HBM)

    conduct, modes, keep, give = pl.pallas_call(
        analyse_kernel,
        out_shape=(block, block, plane, plane),
        in_specs=[hbm] * 7,
        out_specs=(hbm, hbm, vmem, vmem),
        scratch_shapes=[
            pltpu.VMEM((slab, width, width), jnp.float32),
            pltpu.VMEM((slab, width, width), jnp.float32),
            pltpu.VMEM((2, ROWS, width), jnp.float32),
            pltpu.SMEM((1, PHASES), jnp.float32),
            pltpu.VMEM((slab, width, width), jnp.int32),
            pltpu.VMEM((slab, width, width), jnp.float32),
            pltpu.VMEM((2 * width, 2 * width), jnp.bfloat16),
            pltpu.VMEM((2 * width, 2 * width), jnp.bfloat16),
            pltpu.VMEM((width, width), jnp.float32),
            pltpu.VMEM((width, width), jnp.float32),
            pltpu.SemaphoreType.DMA((5,)),
            pltpu.SemaphoreType.DMA((PIECES,)),
            pltpu.SemaphoreType.DMA((PIECES,)),
            pltpu.SemaphoreType.DMA((PIECES,)),
            pltpu.SemaphoreType.DMA((PIECES,)),
        ],
        compiler_params=pltpu.CompilerParams(vmem_limit_bytes=HBM_INPUTS_BYTES),
        name="analyse",
    )(
        material_matrix_diffusivity,
        voxel_material_ids,
        fiber_fraction,
        from_right(tables["basis"].T),
        from_left(tables["basis"]),
        tables["norm"],
        tables["rho"],
    )

    swap = [(i, i ^ 1) for i in range(pencils)]

    def from_chip(array, away):
        perm = [(i, (i + (2 * away if i % 2 == 0 else -2 * away)) % pencils) for i in range(pencils)]
        return lax.ppermute(array, "pencil", perm)

    step, chip_step, scale = tables["step"], tables["chip_step"], tables["scale"]
    chip = lax.ppermute(give, "pencil", swap) + lax.optimization_barrier(step * keep)
    chip, keep, modes, temperature, entry, assign, corners = lax.optimization_barrier(
        (chip, keep, modes, mesh_point_thermal_state, global_entry_position, sample_choice_per_point, element_corner_ids)
    )
    modes = lax.optimization_barrier(modes * tables["norm"])
    kept = lax.optimization_barrier(jnp.where(corner_mask((width, width)), 0.0, keep))
    extra = jnp.concatenate(
        [
            temperature,
            entry.astype(jnp.float32),
            assign.astype(jnp.float32),
            corners.reshape(-1).astype(jnp.float32),
        ]
    )
    extra = jnp.pad(extra, (16, LANES - 16 - extra.shape[0])).reshape(1, LANES)
    coming = [from_chip(chip, away) for away in range(1, chips)] + [chip]
    own = coming[-1]
    for tail in coming[-2::-1]:
        own = tail + chip_step * own
    own = own * scale
    other = lax.ppermute(kept + step * own, "pencil", swap)

    field = (slab + 2, width, width)
    padded = (slab + 2, width + ROWS, width)
    moments = pl.pallas_call(
        moments_kernel,
        out_shape=jax.ShapeDtypeStruct((1, LANES), jnp.float32),
        in_specs=[vmem] * 10,
        out_specs=vmem,
        scratch_shapes=[pltpu.VMEM(s, jnp.float32) for s in (field, field, padded, padded, padded)]
        + [pltpu.VMEM((2 * width, 6 * width), jnp.bfloat16)],
        compiler_params=params,
        name="moments",
    )(
        conduct,
        modes,
        own,
        other,
        extra,
        tables["rho"],
        from_right(tables["basis"]),
        from_right(tables["slope"]),
        from_left(tables["basis"].T),
        from_left(tables["slope"].T),
    )

    table = jnp.broadcast_to(moments, (pencils, LANES))
    table = jnp.sum(lax.all_to_all(table, "pencil", 0, 0, tiled=True), axis=0, keepdims=True)
    table = lax.all_to_all(jnp.broadcast_to(table, (groups, LANES)), "macro", 0, 0, tiled=True)
    flux, nodal = pl.pallas_call(
        lambda *refs: close_kernel(own_nodes, volume, *refs),
        out_shape=(
            jax.ShapeDtypeStruct((1, 3), jnp.float32),
            jax.ShapeDtypeStruct((1, own_nodes), jnp.float32),
        ),
        in_specs=[vmem],
        out_specs=(vmem, vmem),
        name="close",
    )(table)
    return (flux, nodal.reshape(own_nodes))


def solution(mesh):
    in_specs = (
        P("macro", "pencil", None, None),
        P("macro", "pencil", None, None),
        P("macro", None),
        P("macro"),
        P("macro", None),
        P("macro"),
        P("macro"),
    )
    out_specs = (P("macro", None), P("macro"))
    return jax.shard_map(
        on_device, mesh=mesh, in_specs=in_specs, out_specs=out_specs, check_vma=False
    )
```

```python
import math

import jax
import jax.numpy as jnp
import ml_dtypes
import numpy as np
from jax import lax
from jax.experimental import pallas as pl
from jax.experimental.pallas import tpu as pltpu
from jax.sharding import PartitionSpec as P

PHASES = 3
LANES = 128
ROWS = 8
PIECES = 4
VMEM_BYTES = 48 * 1024 * 1024
HBM_INPUTS_BYTES = 56 * 1024 * 1024


def split_table(table):
    high = table.astype(ml_dtypes.bfloat16)
    low = (table - high.astype(np.float64)).astype(ml_dtypes.bfloat16)
    return high, low


def from_right(table):
    high, low = split_table(table)
    return np.block([[high, low], [high, low]])


def from_left(table):
    high, low = split_table(table)
    return np.block([[high, high], [low, low]])


def mode_tables(width, slab):
    half = width // 2
    mode = np.arange(width)
    number = np.where(mode <= half, mode, mode - half)
    angle = 2.0 * np.pi * (number[:, None] * np.arange(width)[None, :] % width) / width
    basis = np.where((mode <= half)[:, None], np.cos(angle), np.sin(angle)) * math.sqrt(2.0 / width)
    basis[0] /= math.sqrt(2.0)
    basis[half] /= math.sqrt(2.0)
    slope = basis - np.roll(basis, 1, axis=1)
    slope[0] = 0.0
    line = 4.0 * np.sin(np.pi * number / width) ** 2
    plane = line[:, None] + line[None, :]
    rho = 1.0 + plane / 2.0 - np.sqrt(plane + plane * plane / 4.0)
    zero = plane == 0.0
    norm = np.where(zero, 0.0, 1.0 / np.where(zero, 1.0, 1.0 / rho - rho))
    scale = np.where(zero, 1.0, 1.0 / np.where(zero, 1.0, 1.0 - rho**width))
    f32 = lambda table: table.astype(np.float32)
    return dict(
        basis=basis,
        slope=slope,
        rho=f32(rho),
        norm=f32(norm),
        step=f32(rho**slab),
        chip_step=f32(rho ** (2 * slab)),
        scale=f32(scale),
    )


def halves(data):
    high = data.astype(jnp.bfloat16)
    low = (data - high.astype(jnp.float32)).astype(jnp.bfloat16)
    return high, low


def beside(data):
    return jnp.concatenate(halves(data), axis=1)


def stacked(data):
    return jnp.concatenate(halves(data), axis=0)


def product(left, right):
    return jnp.dot(left, right, preferred_element_type=jnp.float32)


def corner_mask(shape):
    row = lax.broadcasted_iota(jnp.int32, shape, 0)
    lane = lax.broadcasted_iota(jnp.int32, shape, 1)
    return (row == 0) & (lane == 0)


def analyse_kernel(
    material_hbm, ids_hbm, fiber_hbm, right_hbm, left_hbm, norm_hbm, rho_hbm,
    conduct_hbm, modes_hbm, keep_hbm, give_hbm,
    conduct_ref, modes_ref, keep_ref, give_ref, sums_ref, material_ref, ids_ref, fiber_ref, right_ref, left_ref, norm_ref, rho_ref,
    table_sems, ids_sems, fiber_sems, conduct_sems, modes_sems, tail_sems,
):
    slab, width = fiber_ref.shape[0], fiber_ref.shape[2]
    group = slab // PIECES
    odd = lax.rem(lax.axis_index("pencil"), 2) == 1

    def ids_copy(piece):
        at = pl.ds(piece * group, group)
        return pltpu.make_async_copy(ids_hbm.at[0, at], ids_ref.at[at], ids_sems.at[piece])

    def fiber_copy(piece):
        at = pl.ds(piece * group, group)
        return pltpu.make_async_copy(fiber_hbm.at[0, at], fiber_ref.at[at], fiber_sems.at[piece])

    def conduct_copy(piece):
        at = pl.ds(piece * group, group)
        return pltpu.make_async_copy(conduct_ref.at[at], conduct_hbm.at[at], conduct_sems.at[piece])

    def modes_copy(piece):
        at = pl.ds(piece * group, group)
        return pltpu.make_async_copy(modes_ref.at[at], modes_hbm.at[at], modes_sems.at[piece])

    tables = [
        pltpu.make_async_copy(source, target, table_sems.at[index])
        for index, (source, target) in enumerate(
            (
                (material_hbm, material_ref),
                (right_hbm, right_ref),
                (left_hbm, left_ref),
                (norm_hbm, norm_ref),
                (rho_hbm, rho_ref),
            )
        )
    ]
    tables[0].start()
    ids_copy(0).start()
    fiber_copy(0).start()
    for copy in tables[1:]:
        copy.start()
    for piece in range(1, PIECES):
        ids_copy(piece).start()
        fiber_copy(piece).start()
    sums_ref[...] = jnp.zeros_like(sums_ref)
    for copy in tables:
        copy.wait()

    def along_z(piece):
        ids_copy(piece).wait()
        fiber_copy(piece).wait()
        planes = []
        for part in range(group):
            x = group * piece + part
            ids = ids_ref[x]
            conduct = jnp.where(
                ids == 0, material_ref[0, 0], jnp.where(ids == 1, material_ref[0, 1], material_ref[0, 2])
            )
            conduct = conduct * fiber_ref[x]
            conduct_ref[x] = conduct
            tiles = conduct.reshape(width // ROWS, ROWS, width)
            sums_ref[0] += jnp.sum(tiles, axis=0)
            sums_ref[1] += jnp.sum(tiles * tiles, axis=0)
            planes.append(beside(conduct))
        conduct_copy(piece).start()
        lines = product(jnp.concatenate(planes, axis=0), right_ref[...])
        return lines[:, :width] + lines[:, width:]

    def along_y(piece, lines):
        for part in range(0, group, 2):
            pair = jnp.concatenate(
                [lines[part * width : (part + 1) * width], lines[(part + 1) * width : (part + 2) * width]], axis=1
            )
            modes = product(left_ref[...], stacked(pair))
            modes = modes[:width] + modes[width:]
            modes_ref[group * piece + part] = modes[:, :width]
            modes_ref[group * piece + part + 1] = modes[:, width:]
        modes_copy(piece).start()

    lines = along_z(0)
    for piece in range(1, PIECES):
        ahead = along_z(piece)
        along_y(piece - 1, lines)
        lines = ahead
    along_y(PIECES - 1, lines)
    total = jnp.sum(sums_ref[0])
    total_square = jnp.sum(sums_ref[1])
    rho = rho_ref[...]
    right = modes_ref[0]
    left = modes_ref[slab - 1]
    for x in range(1, slab):
        right = modes_ref[x] + rho * right
        left = modes_ref[slab - 1 - x] + rho * left
    corner = corner_mask(right.shape)
    norm = norm_ref[...]
    right = jnp.where(corner, total, right * norm)
    left = jnp.where(corner, total_square, left * norm)
    tails = [
        pltpu.make_async_copy(give_ref, give_hbm, tail_sems.at[0]),
        pltpu.make_async_copy(keep_ref, keep_hbm, tail_sems.at[1]),
    ]
    give_ref[...] = jnp.where(odd, right, left)
    tails[0].start()
    keep_ref[...] = jnp.where(odd, left, right)
    tails[1].start()
    for copy in tails:
        copy.wait()
    for piece in range(PIECES):
        conduct_copy(piece).wait()
        modes_copy(piece).wait()


def moments_kernel(
    conduct_ref, modes_ref, own_ref, other_ref, extra_ref, rho_ref,
    right_basis_ref, right_slope_ref, left_basis_ref, left_slope_ref,
    out_ref, potential_ref, rise_ref, px_ref, py_ref, pz_ref, lines_ref,
):
    slab, width = conduct_ref.shape[0], conduct_ref.shape[2]
    volume = float(width**3)
    pencil = lax.axis_index("pencil")
    odd = lax.rem(pencil, 2) == 1

    corner = corner_mask((width, width))
    first_plane = jnp.where(odd, other_ref[...], own_ref[...])
    second_plane = jnp.where(odd, own_ref[...], other_ref[...])
    first = jnp.sum(jnp.where(corner, first_plane, 0.0)[:ROWS])
    second = jnp.sum(jnp.where(corner, second_plane, 0.0)[:ROWS])
    mean = first / volume
    rho = rho_ref[...]
    behind = jnp.where(corner, 0.0, second_plane)
    potential_ref[slab] = behind
    behind = rho * behind
    potential_ref[slab - 1] = behind
    for x in range(slab - 2, -1, -1):
        behind = rho * (modes_ref[x + 1] + behind)
        potential_ref[x] = behind
    ahead = jnp.where(corner, 0.0, first_plane)
    last = ahead + rho * (modes_ref[0] + behind)
    for x in range(slab + 1):
        ahead = rho * ahead
        if x < slab:
            ahead = ahead + modes_ref[x]
        here = ahead + potential_ref[x]
        potential_ref[x] = here
        rise_ref[x] = here - last
        last = here
    potential_ref[slab + 1] = last
    rise_ref[slab + 1] = last

    def put(ref, x, plane):
        ref[x, :width] = plane
        ref[x, width:] = plane[:ROWS]

    def along_z(pair):
        planes = [2 * pair, 2 * pair + 1]
        along = jnp.concatenate([beside(potential_ref[x]) for x in planes], axis=0)
        rise = product(jnp.concatenate([beside(rise_ref[x]) for x in planes], axis=0), right_basis_ref[...])
        slope = product(along, right_slope_ref[...])
        plain = product(along, right_basis_ref[...])
        for place, lines in enumerate((slope, rise, plain)):
            high, low = halves(lines[:, :width] + lines[:, width:])
            for part in range(2):
                rows = slice(part * width, (part + 1) * width)
                lanes = pl.ds((2 * part + place if place < 2 else 4 + part) * width, width)
                lines_ref[:width, lanes] = high[rows]
                lines_ref[width:, lanes] = low[rows]

    def along_y(pair):
        third = product(left_slope_ref[...], lines_ref[:, 4 * width :])
        third = third[:width] + third[width:]
        for part in range(2):
            both = product(left_basis_ref[...], lines_ref[:, 2 * part * width : 2 * (part + 1) * width])
            both = both[:width] + both[width:]
            put(pz_ref, 2 * pair + part, both[:, :width])
            put(px_ref, 2 * pair + part, both[:, width:])
            put(py_ref, 2 * pair + part, third[:, part * width : (part + 1) * width])

    pairs = slab // 2 + 1

    def lines_only(step, carry):
        along_z(step)
        return carry

    def warm(step, carry):
        along_y(step - 1)
        along_z(step)
        return carry

    def plane(step, totals, products=2):
        totals = list(totals)
        for place in range(2 * (width // ROWS)):
            x = 2 * (step - 3) + place // (width // ROWS)
            chunk = place % (width // ROWS)
            at = pl.ds(chunk * ROWS, ROWS)
            down = pl.ds(chunk * ROWS + 1, ROWS)
            conduct = conduct_ref[x, at]
            px, py, pz = px_ref[x, at], py_ref[x, at], pz_ref[x, at]
            turn = lambda field: pltpu.roll(field, width - 1, 1) - field
            e_yx, e_zx = px_ref[x, down] - px, turn(px)
            e_xy, e_yy, e_zy = py_ref[x + 1, at] - py, py_ref[x, down] - py, turn(py)
            e_xz, e_yz, e_zz = pz_ref[x + 1, at] - pz, pz_ref[x, down] - pz, turn(pz)
            e_xx = (mean - conduct) - (e_yy + e_zz)
            e = ((e_xx, e_yx, e_zx), (e_xy, e_yy, e_zy), (e_xz, e_yz, e_zz))
            at_entry = 0
            for i in range(3):
                for j in range(i, 3):
                    term = e[i][0] * e[j][0] + e[i][1] * e[j][1] + e[i][2] * e[j][2]
                    totals[at_entry] = totals[at_entry] + term
                    totals[6 + at_entry] = totals[6 + at_entry] + conduct * term
                    at_entry += 1
        if products > 0:
            along_y(step - 1)
        if products > 1:
            along_z(step)
        return tuple(totals)

    nothing = jnp.zeros((ROWS, width), jnp.float32)
    lax.fori_loop(0, 1, lines_only, 0)
    lax.fori_loop(1, 3, warm, 0)
    totals = lax.fori_loop(3, pairs, plane, (nothing,) * 12)
    totals = lax.fori_loop(pairs, pairs + 1, lambda step, t: plane(step, t, 1), totals)
    totals = lax.fori_loop(pairs + 1, pairs + 2, lambda step, t: plane(step, t, 0), totals)
    lines = [jnp.sum(total, axis=0, keepdims=True) for total in totals]
    lines = jnp.concatenate(lines + [jnp.zeros((4, width), jnp.float32)], axis=0)
    column = jnp.sum(lines, axis=1, keepdims=True)
    row = lax.broadcasted_iota(jnp.int32, (16, width), 0)
    lane = lax.broadcasted_iota(jnp.int32, (16, width), 1)
    once = jnp.where(pencil == 0, 1.0, 0.0)
    column = jnp.where(row == 12, first * once, jnp.where(row == 13, second * once, column))
    out_ref[...] = jnp.sum(jnp.where(row == lane, column, 0.0), axis=0, keepdims=True) + extra_ref[...] * once


def close_kernel(nodes_own, volume, table_ref, flux_ref, nodal_ref):
    points = table_ref.shape[0]
    macro = lax.axis_index("macro")
    table = table_ref[...]
    lane = lax.broadcasted_iota(jnp.int32, (points, LANES), 1)
    row = lax.broadcasted_iota(jnp.int32, (points, LANES), 0)
    column = lambda index: table[:, index : index + 1]

    temperature = jnp.zeros((points, LANES), jnp.float32)
    node_of = jnp.zeros((points, LANES), jnp.float32)
    mine = (macro * nodes_own + lane).astype(jnp.float32)
    for node in range(nodes_own):
        at = row * nodes_own + node
        temperature = jnp.where(lane == at, column(16 + node), temperature)
        node_of = jnp.where(column(16 + nodes_own + node) == mine, at.astype(jnp.float32), node_of)
    temperature = jnp.sum(temperature, axis=0, keepdims=True)
    node_of = jnp.sum(node_of, axis=0, keepdims=True)
    node_of = jnp.where(lane[:1] < nodes_own, node_of, -1.0)
    assign = column(16 + 2 * nodes_own)
    corners = [column(17 + 2 * nodes_own + corner) for corner in range(8)]
    theta = []
    for corner in range(8):
        pick = lane.astype(jnp.float32) == corners[corner]
        theta.append(jnp.sum(jnp.where(pick, temperature, 0.0), axis=1, keepdims=True))
    sign = lambda corner, axis: 2.0 * (corner >> axis & 1) - 1.0
    gradient = [sum(sign(a, d) * theta[a] for a in range(8)) / 4.0 for d in range(3)]
    heat = sum(theta) / 8.0
    chosen = jnp.where(
        lax.broadcasted_iota(jnp.int32, (points, points), 1).astype(jnp.float32) == assign, 1.0, 0.0
    )
    high, rest = halves(table)
    low = (table - high.astype(jnp.float32) - rest.astype(jnp.float32)).astype(jnp.bfloat16)
    picked = product(chosen.astype(jnp.bfloat16), jnp.concatenate([high, rest, low], axis=1))
    moments = (picked[:, :LANES] + (picked[:, LANES : 2 * LANES] + picked[:, 2 * LANES :])) * (1.0 / volume)
    moment = lambda index: moments[:, index : index + 1]
    mean, mean_square = moment(12), moment(13)
    radiative = heat * heat * heat
    inverse_k = lax.rsqrt(mean_square + 2.0 * radiative * mean + radiative * radiative)
    order = ((0, 1, 2), (1, 3, 4), (2, 4, 5))
    flux = []
    for d in range(3):
        plain = sum(moment(order[d][j]) * gradient[j] for j in range(3))
        weighted = sum(moment(6 + order[d][j]) * gradient[j] for j in range(3))
        flux.append(
            gradient[d] * (mean + radiative)
            + weighted * (inverse_k * inverse_k)
            - plain * (inverse_k * (2.0 - radiative * inverse_k))
        )
    spread = jnp.zeros((points, LANES), jnp.float32)
    for d in range(3):
        spread = jnp.where(lane == d, flux[d], spread)
    flux_ref[...] = jnp.sum(jnp.where(row == macro, spread, 0.0), axis=0, keepdims=True)[:, :3]
    assembled = jnp.zeros((points, LANES), jnp.float32)
    for corner in range(8):
        residual = sum(sign(corner, d) * flux[d] for d in range(3)) / 4.0
        assembled = assembled + jnp.where(corners[corner] == node_of, residual, 0.0)
    nodal_ref[...] = jnp.sum(assembled, axis=0, keepdims=True)[:, :nodes_own]


def on_device(
    voxel_material_ids,
    fiber_fraction,
    material_matrix_diffusivity,
    mesh_point_thermal_state,
    element_corner_ids,
    global_entry_position,
    sample_choice_per_point,
):
    slab = fiber_fraction.shape[1]
    width = fiber_fraction.shape[3]
    volume = float(width**3)
    own_nodes = mesh_point_thermal_state.shape[0]
    pencils = lax.axis_size("pencil")
    chips = pencils // 2
    groups = lax.axis_size("macro")
    tables = mode_tables(width, slab)
    plane = jax.ShapeDtypeStruct((width, width), jnp.float32)
    block = jax.ShapeDtypeStruct((slab, width, width), jnp.float32)
    params = pltpu.CompilerParams(vmem_limit_bytes=VMEM_BYTES)
    vmem = pl.BlockSpec(memory_space=pltpu.VMEM)
    hbm = pl.BlockSpec(memory_space=pltpu.HBM)

    conduct, modes, keep, give = pl.pallas_call(
        analyse_kernel,
        out_shape=(block, block, plane, plane),
        in_specs=[hbm] * 7,
        out_specs=(hbm,) * 4,
        scratch_shapes=[
            pltpu.VMEM((slab, width, width), jnp.float32),
            pltpu.VMEM((slab, width, width), jnp.float32),
            pltpu.VMEM((width, width), jnp.float32),
            pltpu.VMEM((width, width), jnp.float32),
            pltpu.VMEM((2, ROWS, width), jnp.float32),
            pltpu.SMEM((1, PHASES), jnp.float32),
            pltpu.VMEM((slab, width, width), jnp.int32),
            pltpu.VMEM((slab, width, width), jnp.float32),
            pltpu.VMEM((2 * width, 2 * width), jnp.bfloat16),
            pltpu.VMEM((2 * width, 2 * width), jnp.bfloat16),
            pltpu.VMEM((width, width), jnp.float32),
            pltpu.VMEM((width, width), jnp.float32),
            pltpu.SemaphoreType.DMA((5,)),
            pltpu.SemaphoreType.DMA((PIECES,)),
            pltpu.SemaphoreType.DMA((PIECES,)),
            pltpu.SemaphoreType.DMA((PIECES,)),
            pltpu.SemaphoreType.DMA((PIECES,)),
            pltpu.SemaphoreType.DMA((2,)),
        ],
        compiler_params=pltpu.CompilerParams(vmem_limit_bytes=HBM_INPUTS_BYTES),
        name="analyse",
    )(
        material_matrix_diffusivity,
        voxel_material_ids,
        fiber_fraction,
        from_right(tables["basis"].T),
        from_left(tables["basis"]),
        tables["norm"],
        tables["rho"],
    )

    swap = [(i, i ^ 1) for i in range(pencils)]

    def from_chip(array, away):
        perm = [(i, (i + (2 * away if i % 2 == 0 else -2 * away)) % pencils) for i in range(pencils)]
        return lax.ppermute(array, "pencil", perm)

    step, chip_step = tables["step"], tables["chip_step"]
    chip = lax.ppermute(give, "pencil", swap) + lax.optimization_barrier(step * keep)
    chip, keep, modes, temperature, entry, assign, corners = lax.optimization_barrier(
        (chip, keep, modes, mesh_point_thermal_state, global_entry_position, sample_choice_per_point, element_corner_ids)
    )
    modes = lax.optimization_barrier(modes * tables["norm"])
    kept = lax.optimization_barrier(jnp.where(corner_mask((width, width)), 0.0, keep))
    extra = jnp.concatenate(
        [
            temperature,
            entry.astype(jnp.float32),
            assign.astype(jnp.float32),
            corners.reshape(-1).astype(jnp.float32),
        ]
    )
    extra = jnp.pad(extra, (16, LANES - 16 - extra.shape[0])).reshape(1, LANES)
    half = chips // 2
    powers = [tables["scale"], tables["scale"] * chip_step]
    while len(powers) < chips:
        powers.append(powers[-1] * chip_step)
    own = lax.optimization_barrier(powers[half - 1] * from_chip(chip, half) + powers[-1] * chip)
    for away in range(1, chips):
        if away != half:
            own = own + powers[away - 1] * from_chip(chip, away)
    other = lax.ppermute(kept + step * own, "pencil", swap)

    field = (slab + 2, width, width)
    padded = (slab + 2, width + ROWS, width)
    moments = pl.pallas_call(
        moments_kernel,
        out_shape=jax.ShapeDtypeStruct((1, LANES), jnp.float32),
        in_specs=[vmem] * 10,
        out_specs=vmem,
        scratch_shapes=[pltpu.VMEM(s, jnp.float32) for s in (field, field, padded, padded, padded)]
        + [pltpu.VMEM((2 * width, 6 * width), jnp.bfloat16)],
        compiler_params=params,
        name="moments",
    )(
        conduct,
        modes,
        own,
        other,
        extra,
        tables["rho"],
        from_right(tables["basis"]),
        from_right(tables["slope"]),
        from_left(tables["basis"].T),
        from_left(tables["slope"].T),
    )

    table = jnp.broadcast_to(moments, (pencils, LANES))
    table = jnp.sum(lax.all_to_all(table, "pencil", 0, 0, tiled=True), axis=0, keepdims=True)
    table = lax.all_to_all(jnp.broadcast_to(table, (groups, LANES)), "macro", 0, 0, tiled=True)
    flux, nodal = pl.pallas_call(
        lambda *refs: close_kernel(own_nodes, volume, *refs),
        out_shape=(
            jax.ShapeDtypeStruct((1, 3), jnp.float32),
            jax.ShapeDtypeStruct((1, own_nodes), jnp.float32),
        ),
        in_specs=[vmem],
        out_specs=(vmem, vmem),
        name="close",
    )(table)
    return (flux, nodal.reshape(own_nodes))


def solution(mesh):
    in_specs = (
        P("macro", "pencil", None, None),
        P("macro", "pencil", None, None),
        P("macro", None),
        P("macro"),
        P("macro", None),
        P("macro"),
        P("macro"),
    )
    out_specs = (P("macro", None), P("macro"))
    return jax.shard_map(
        on_device, mesh=mesh, in_specs=in_specs, out_specs=out_specs, check_vma=False
    )
```

```python
import math

import jax
import jax.numpy as jnp
import ml_dtypes
import numpy as np
from jax import lax
from jax.experimental import pallas as pl
from jax.experimental.pallas import tpu as pltpu
from jax.sharding import PartitionSpec as P

PHASES = 3
LANES = 128
ROWS = 8
PIECES = 4
VMEM_BYTES = 48 * 1024 * 1024
HBM_INPUTS_BYTES = 56 * 1024 * 1024


def split_table(table):
    high = table.astype(ml_dtypes.bfloat16)
    low = (table - high.astype(np.float64)).astype(ml_dtypes.bfloat16)
    return high, low


def from_right(table):
    high, low = split_table(table)
    return np.block([[high, low], [high, low]])


def from_left(table):
    high, low = split_table(table)
    return np.block([[high, high], [low, low]])


def mode_tables(width, slab):
    half = width // 2
    mode = np.arange(width)
    number = np.where(mode <= half, mode, mode - half)
    angle = 2.0 * np.pi * (number[:, None] * np.arange(width)[None, :] % width) / width
    basis = np.where((mode <= half)[:, None], np.cos(angle), np.sin(angle)) * math.sqrt(2.0 / width)
    basis[0] /= math.sqrt(2.0)
    basis[half] /= math.sqrt(2.0)
    slope = basis - np.roll(basis, 1, axis=1)
    slope[0] = 0.0
    line = 4.0 * np.sin(np.pi * number / width) ** 2
    plane = line[:, None] + line[None, :]
    rho = 1.0 + plane / 2.0 - np.sqrt(plane + plane * plane / 4.0)
    zero = plane == 0.0
    norm = np.where(zero, 0.0, 1.0 / np.where(zero, 1.0, 1.0 / rho - rho))
    scale = np.where(zero, 1.0, 1.0 / np.where(zero, 1.0, 1.0 - rho**width))
    f32 = lambda table: table.astype(np.float32)
    return dict(
        basis=basis,
        slope=slope,
        rho=f32(rho),
        norm=f32(norm),
        step=f32(rho**slab),
        chip_step=f32(rho ** (2 * slab)),
        scale=f32(scale),
    )


def halves(data):
    high = data.astype(jnp.bfloat16)
    low = (data - high.astype(jnp.float32)).astype(jnp.bfloat16)
    return high, low


def beside(data):
    return jnp.concatenate(halves(data), axis=1)


def stacked(data):
    return jnp.concatenate(halves(data), axis=0)


def product(left, right):
    return jnp.dot(left, right, preferred_element_type=jnp.float32)


def corner_mask(shape):
    row = lax.broadcasted_iota(jnp.int32, shape, 0)
    lane = lax.broadcasted_iota(jnp.int32, shape, 1)
    return (row == 0) & (lane == 0)


def analyse_kernel(
    material_hbm, ids_hbm, fiber_hbm, right_hbm, left_hbm, norm_hbm, rho_hbm,
    conduct_hbm, modes_hbm, keep_hbm, give_hbm,
    conduct_ref, modes_ref, keep_ref, give_ref, sums_ref, material_ref, ids_ref, fiber_ref, right_ref, left_ref, norm_ref, rho_ref,
    table_sems, ids_sems, fiber_sems, conduct_sems, modes_sems, tail_sems,
):
    slab, width = fiber_ref.shape[0], fiber_ref.shape[2]
    group = slab // PIECES
    odd = lax.rem(lax.axis_index("pencil"), 2) == 1

    def ids_copy(piece):
        at = pl.ds(piece * group, group)
        return pltpu.make_async_copy(ids_hbm.at[0, at], ids_ref.at[at], ids_sems.at[piece])

    def fiber_copy(piece):
        at = pl.ds(piece * group, group)
        return pltpu.make_async_copy(fiber_hbm.at[0, at], fiber_ref.at[at], fiber_sems.at[piece])

    def conduct_copy(piece):
        at = pl.ds(piece * group, group)
        return pltpu.make_async_copy(conduct_ref.at[at], conduct_hbm.at[at], conduct_sems.at[piece])

    def modes_copy(piece):
        at = pl.ds(piece * group, group)
        return pltpu.make_async_copy(modes_ref.at[at], modes_hbm.at[at], modes_sems.at[piece])

    tables = [
        pltpu.make_async_copy(source, target, table_sems.at[index])
        for index, (source, target) in enumerate(
            (
                (material_hbm, material_ref),
                (right_hbm, right_ref),
                (left_hbm, left_ref),
                (norm_hbm, norm_ref),
                (rho_hbm, rho_ref),
            )
        )
    ]
    tables[0].start()
    ids_copy(0).start()
    fiber_copy(0).start()
    for copy in tables[1:]:
        copy.start()
    for piece in range(1, PIECES):
        ids_copy(piece).start()
        fiber_copy(piece).start()
    sums_ref[...] = jnp.zeros_like(sums_ref)
    tables[0].wait()

    def along_z(piece):
        if piece == 0:
            for each in range(PIECES):
                ids_copy(each).wait()
                fiber_copy(each).wait()
            for copy in tables[1:]:
                copy.wait()
        planes = []
        for part in range(group):
            x = group * piece + part
            ids = ids_ref[x]
            conduct = jnp.where(
                ids == 0, material_ref[0, 0], jnp.where(ids == 1, material_ref[0, 1], material_ref[0, 2])
            )
            conduct = conduct * fiber_ref[x]
            conduct_ref[x] = conduct
            tiles = conduct.reshape(width // ROWS, ROWS, width)
            sums_ref[0] += jnp.sum(tiles, axis=0)
            sums_ref[1] += jnp.sum(tiles * tiles, axis=0)
            planes.append(beside(conduct))
        conduct_copy(piece).start()
        lines = product(jnp.concatenate(planes, axis=0), right_ref[...])
        return lines[:, :width] + lines[:, width:]

    def along_y(piece, lines):
        for part in range(0, group, 2):
            pair = jnp.concatenate(
                [lines[part * width : (part + 1) * width], lines[(part + 1) * width : (part + 2) * width]], axis=1
            )
            modes = product(left_ref[...], stacked(pair))
            modes = modes[:width] + modes[width:]
            modes_ref[group * piece + part] = modes[:, :width]
            modes_ref[group * piece + part + 1] = modes[:, width:]
        modes_copy(piece).start()

    lines = along_z(0)
    for piece in range(1, PIECES):
        ahead = along_z(piece)
        along_y(piece - 1, lines)
        lines = ahead
    along_y(PIECES - 1, lines)
    total = jnp.sum(sums_ref[0])
    total_square = jnp.sum(sums_ref[1])
    rho = rho_ref[...]
    right = modes_ref[0]
    left = modes_ref[slab - 1]
    for x in range(1, slab):
        right = modes_ref[x] + rho * right
        left = modes_ref[slab - 1 - x] + rho * left
    corner = corner_mask(right.shape)
    norm = norm_ref[...]
    right = jnp.where(corner, total, right * norm)
    left = jnp.where(corner, total_square, left * norm)
    tails = [
        pltpu.make_async_copy(give_ref, give_hbm, tail_sems.at[0]),
        pltpu.make_async_copy(keep_ref, keep_hbm, tail_sems.at[1]),
    ]
    give_ref[...] = jnp.where(odd, right, left)
    tails[0].start()
    keep_ref[...] = jnp.where(odd, left, right)
    tails[1].start()
    for copy in tails:
        copy.wait()
    for piece in range(PIECES):
        conduct_copy(piece).wait()
        modes_copy(piece).wait()


def moments_kernel(
    conduct_ref, modes_ref, own_ref, other_ref, extra_ref, rho_ref,
    right_basis_ref, right_slope_ref, left_basis_ref, left_slope_ref,
    out_ref, potential_ref, rise_ref, px_ref, py_ref, pz_ref, lines_ref,
):
    slab, width = conduct_ref.shape[0], conduct_ref.shape[2]
    volume = float(width**3)
    pencil = lax.axis_index("pencil")
    odd = lax.rem(pencil, 2) == 1

    corner = corner_mask((width, width))
    first_plane = jnp.where(odd, other_ref[...], own_ref[...])
    second_plane = jnp.where(odd, own_ref[...], other_ref[...])
    first = jnp.sum(jnp.where(corner, first_plane, 0.0)[:ROWS])
    second = jnp.sum(jnp.where(corner, second_plane, 0.0)[:ROWS])
    mean = first / volume
    rho = rho_ref[...]
    behind = jnp.where(corner, 0.0, second_plane)
    potential_ref[slab] = behind
    behind = rho * behind
    potential_ref[slab - 1] = behind
    for x in range(slab - 2, -1, -1):
        behind = rho * (modes_ref[x + 1] + behind)
        potential_ref[x] = behind
    ahead = jnp.where(corner, 0.0, first_plane)
    last = ahead + rho * (modes_ref[0] + behind)
    for x in range(slab + 1):
        ahead = rho * ahead
        if x < slab:
            ahead = ahead + modes_ref[x]
        here = ahead + potential_ref[x]
        potential_ref[x] = here
        rise_ref[x] = here - last
        last = here
    potential_ref[slab + 1] = last
    rise_ref[slab + 1] = last

    def put(ref, x, plane):
        ref[x, :width] = plane
        ref[x, width:] = plane[:ROWS]

    def along_z(pair):
        planes = [2 * pair, 2 * pair + 1]
        along = jnp.concatenate([beside(potential_ref[x]) for x in planes], axis=0)
        rise = product(jnp.concatenate([beside(rise_ref[x]) for x in planes], axis=0), right_basis_ref[...])
        slope = product(along, right_slope_ref[...])
        plain = product(along, right_basis_ref[...])
        for place, lines in enumerate((slope, rise, plain)):
            high, low = halves(lines[:, :width] + lines[:, width:])
            for part in range(2):
                rows = slice(part * width, (part + 1) * width)
                lanes = pl.ds((2 * part + place if place < 2 else 4 + part) * width, width)
                lines_ref[:width, lanes] = high[rows]
                lines_ref[width:, lanes] = low[rows]

    def along_y(pair):
        third = product(left_slope_ref[...], lines_ref[:, 4 * width :])
        third = third[:width] + third[width:]
        for part in range(2):
            both = product(left_basis_ref[...], lines_ref[:, 2 * part * width : 2 * (part + 1) * width])
            both = both[:width] + both[width:]
            put(pz_ref, 2 * pair + part, both[:, :width])
            put(px_ref, 2 * pair + part, both[:, width:])
            put(py_ref, 2 * pair + part, third[:, part * width : (part + 1) * width])

    pairs = slab // 2 + 1

    def differences(pair, totals):
        totals = list(totals)
        for place in range(2 * (width // ROWS)):
            x = 2 * pair + place // (width // ROWS)
            chunk = place % (width // ROWS)
            at = pl.ds(chunk * ROWS, ROWS)
            down = pl.ds(chunk * ROWS + 1, ROWS)
            conduct = conduct_ref[x, at]
            px, py, pz = px_ref[x, at], py_ref[x, at], pz_ref[x, at]
            turn = lambda field: pltpu.roll(field, width - 1, 1) - field
            e_yx, e_zx = px_ref[x, down] - px, turn(px)
            e_xy, e_yy, e_zy = py_ref[x + 1, at] - py, py_ref[x, down] - py, turn(py)
            e_xz, e_yz, e_zz = pz_ref[x + 1, at] - pz, pz_ref[x, down] - pz, turn(pz)
            e_xx = (mean - conduct) - (e_yy + e_zz)
            e = ((e_xx, e_yx, e_zx), (e_xy, e_yy, e_zy), (e_xz, e_yz, e_zz))
            at_entry = 0
            for i in range(3):
                for j in range(i, 3):
                    term = e[i][0] * e[j][0] + e[i][1] * e[j][1] + e[i][2] * e[j][2]
                    totals[at_entry] = totals[at_entry] + term
                    totals[6 + at_entry] = totals[6 + at_entry] + conduct * term
                    at_entry += 1
        return tuple(totals)

    nothing = jnp.zeros((ROWS, width), jnp.float32)
    totals = (nothing,) * 12
    for step in range(pairs + 2):
        if step >= 3:
            totals = differences(step - 3, totals)
        if 1 <= step <= pairs:
            along_y(step - 1)
        if step < pairs:
            along_z(step)
    lines = [jnp.sum(total, axis=0, keepdims=True) for total in totals]
    lines = jnp.concatenate(lines + [jnp.zeros((4, width), jnp.float32)], axis=0)
    column = jnp.sum(lines, axis=1, keepdims=True)
    row = lax.broadcasted_iota(jnp.int32, (16, width), 0)
    lane = lax.broadcasted_iota(jnp.int32, (16, width), 1)
    once = jnp.where(pencil == 0, 1.0, 0.0)
    column = jnp.where(row == 12, first * once, jnp.where(row == 13, second * once, column))
    out_ref[...] = jnp.sum(jnp.where(row == lane, column, 0.0), axis=0, keepdims=True) + extra_ref[...] * once


def close_kernel(nodes_own, volume, table_ref, flux_ref, nodal_ref):
    points = table_ref.shape[0]
    macro = lax.axis_index("macro")
    table = table_ref[...]
    lane = lax.broadcasted_iota(jnp.int32, (points, LANES), 1)
    row = lax.broadcasted_iota(jnp.int32, (points, LANES), 0)
    column = lambda index: table[:, index : index + 1]

    temperature = jnp.zeros((points, LANES), jnp.float32)
    node_of = jnp.zeros((points, LANES), jnp.float32)
    mine = (macro * nodes_own + lane).astype(jnp.float32)
    for node in range(nodes_own):
        at = row * nodes_own + node
        temperature = jnp.where(lane == at, column(16 + node), temperature)
        node_of = jnp.where(column(16 + nodes_own + node) == mine, at.astype(jnp.float32), node_of)
    temperature = jnp.sum(temperature, axis=0, keepdims=True)
    node_of = jnp.sum(node_of, axis=0, keepdims=True)
    node_of = jnp.where(lane[:1] < nodes_own, node_of, -1.0)
    assign = column(16 + 2 * nodes_own)
    corners = [column(17 + 2 * nodes_own + corner) for corner in range(8)]
    theta = []
    for corner in range(8):
        pick = lane.astype(jnp.float32) == corners[corner]
        theta.append(jnp.sum(jnp.where(pick, temperature, 0.0), axis=1, keepdims=True))
    sign = lambda corner, axis: 2.0 * (corner >> axis & 1) - 1.0
    gradient = [sum(sign(a, d) * theta[a] for a in range(8)) / 4.0 for d in range(3)]
    heat = sum(theta) / 8.0
    chosen = jnp.where(
        lax.broadcasted_iota(jnp.int32, (points, points), 1).astype(jnp.float32) == assign, 1.0, 0.0
    )
    high, rest = halves(table)
    low = (table - high.astype(jnp.float32) - rest.astype(jnp.float32)).astype(jnp.bfloat16)
    picked = product(chosen.astype(jnp.bfloat16), jnp.concatenate([high, rest, low], axis=1))
    moments = (picked[:, :LANES] + (picked[:, LANES : 2 * LANES] + picked[:, 2 * LANES :])) * (1.0 / volume)
    moment = lambda index: moments[:, index : index + 1]
    mean, mean_square = moment(12), moment(13)
    radiative = heat * heat * heat
    inverse_k = lax.rsqrt(mean_square + 2.0 * radiative * mean + radiative * radiative)
    order = ((0, 1, 2), (1, 3, 4), (2, 4, 5))
    flux = []
    for d in range(3):
        plain = sum(moment(order[d][j]) * gradient[j] for j in range(3))
        weighted = sum(moment(6 + order[d][j]) * gradient[j] for j in range(3))
        flux.append(
            gradient[d] * (mean + radiative)
            + weighted * (inverse_k * inverse_k)
            - plain * (inverse_k * (2.0 - radiative * inverse_k))
        )
    spread = jnp.zeros((points, LANES), jnp.float32)
    for d in range(3):
        spread = jnp.where(lane == d, flux[d], spread)
    flux_ref[...] = jnp.sum(jnp.where(row == macro, spread, 0.0), axis=0, keepdims=True)[:, :3]
    assembled = jnp.zeros((points, LANES), jnp.float32)
    for corner in range(8):
        residual = sum(sign(corner, d) * flux[d] for d in range(3)) / 4.0
        assembled = assembled + jnp.where(corners[corner] == node_of, residual, 0.0)
    nodal_ref[...] = jnp.sum(assembled, axis=0, keepdims=True)[:, :nodes_own]


def on_device(
    voxel_material_ids,
    fiber_fraction,
    material_matrix_diffusivity,
    mesh_point_thermal_state,
    element_corner_ids,
    global_entry_position,
    sample_choice_per_point,
):
    slab = fiber_fraction.shape[1]
    width = fiber_fraction.shape[3]
    volume = float(width**3)
    own_nodes = mesh_point_thermal_state.shape[0]
    pencils = lax.axis_size("pencil")
    chips = pencils // 2
    groups = lax.axis_size("macro")
    tables = mode_tables(width, slab)
    plane = jax.ShapeDtypeStruct((width, width), jnp.float32)
    block = jax.ShapeDtypeStruct((slab, width, width), jnp.float32)
    params = pltpu.CompilerParams(vmem_limit_bytes=VMEM_BYTES)
    vmem = pl.BlockSpec(memory_space=pltpu.VMEM)
    hbm = pl.BlockSpec(memory_space=pltpu.HBM)

    conduct, modes, keep, give = pl.pallas_call(
        analyse_kernel,
        out_shape=(block, block, plane, plane),
        in_specs=[hbm] * 7,
        out_specs=(hbm,) * 4,
        scratch_shapes=[
            pltpu.VMEM((slab, width, width), jnp.float32),
            pltpu.VMEM((slab, width, width), jnp.float32),
            pltpu.VMEM((width, width), jnp.float32),
            pltpu.VMEM((width, width), jnp.float32),
            pltpu.VMEM((2, ROWS, width), jnp.float32),
            pltpu.SMEM((1, PHASES), jnp.float32),
            pltpu.VMEM((slab, width, width), jnp.int32),
            pltpu.VMEM((slab, width, width), jnp.float32),
            pltpu.VMEM((2 * width, 2 * width), jnp.bfloat16),
            pltpu.VMEM((2 * width, 2 * width), jnp.bfloat16),
            pltpu.VMEM((width, width), jnp.float32),
            pltpu.VMEM((width, width), jnp.float32),
            pltpu.SemaphoreType.DMA((5,)),
            pltpu.SemaphoreType.DMA((PIECES,)),
            pltpu.SemaphoreType.DMA((PIECES,)),
            pltpu.SemaphoreType.DMA((PIECES,)),
            pltpu.SemaphoreType.DMA((PIECES,)),
            pltpu.SemaphoreType.DMA((2,)),
        ],
        compiler_params=pltpu.CompilerParams(vmem_limit_bytes=HBM_INPUTS_BYTES),
        name="analyse",
    )(
        material_matrix_diffusivity,
        voxel_material_ids,
        fiber_fraction,
        from_right(tables["basis"].T),
        from_left(tables["basis"]),
        tables["norm"],
        tables["rho"],
    )

    swap = [(i, i ^ 1) for i in range(pencils)]

    def from_chip(array, away):
        perm = [(i, (i + (2 * away if i % 2 == 0 else -2 * away)) % pencils) for i in range(pencils)]
        return lax.ppermute(array, "pencil", perm)

    step, chip_step = tables["step"], tables["chip_step"]
    chip = lax.ppermute(give, "pencil", swap) + lax.optimization_barrier(step * keep)
    chip, keep, modes, temperature, entry, assign, corners = lax.optimization_barrier(
        (chip, keep, modes, mesh_point_thermal_state, global_entry_position, sample_choice_per_point, element_corner_ids)
    )
    modes = lax.optimization_barrier(modes * tables["norm"])
    kept = lax.optimization_barrier(jnp.where(corner_mask((width, width)), 0.0, keep))
    extra = jnp.concatenate(
        [
            temperature,
            entry.astype(jnp.float32),
            assign.astype(jnp.float32),
            corners.reshape(-1).astype(jnp.float32),
        ]
    )
    extra = jnp.pad(extra, (16, LANES - 16 - extra.shape[0])).reshape(1, LANES)
    half = chips // 2
    powers = [tables["scale"], tables["scale"] * chip_step]
    while len(powers) < chips:
        powers.append(powers[-1] * chip_step)
    own = lax.optimization_barrier(powers[half - 1] * from_chip(chip, half) + powers[-1] * chip)
    for away in range(1, chips):
        if away != half:
            own = own + powers[away - 1] * from_chip(chip, away)
    other = lax.ppermute(kept + step * own, "pencil", swap)

    field = (slab + 2, width, width)
    padded = (slab + 2, width + ROWS, width)
    moments = pl.pallas_call(
        moments_kernel,
        out_shape=jax.ShapeDtypeStruct((1, LANES), jnp.float32),
        in_specs=[vmem] * 10,
        out_specs=vmem,
        scratch_shapes=[pltpu.VMEM(s, jnp.float32) for s in (field, field, padded, padded, padded)]
        + [pltpu.VMEM((2 * width, 6 * width), jnp.bfloat16)],
        compiler_params=params,
        name="moments",
    )(
        conduct,
        modes,
        own,
        other,
        extra,
        tables["rho"],
        from_right(tables["basis"]),
        from_right(tables["slope"]),
        from_left(tables["basis"].T),
        from_left(tables["slope"].T),
    )

    table = jnp.broadcast_to(moments, (pencils, LANES))
    table = jnp.sum(lax.all_to_all(table, "pencil", 0, 0, tiled=True), axis=0, keepdims=True)
    table = lax.all_to_all(jnp.broadcast_to(table, (groups, LANES)), "macro", 0, 0, tiled=True)
    flux, nodal = pl.pallas_call(
        lambda *refs: close_kernel(own_nodes, volume, *refs),
        out_shape=(
            jax.ShapeDtypeStruct((1, 3), jnp.float32),
            jax.ShapeDtypeStruct((1, own_nodes), jnp.float32),
        ),
        in_specs=[vmem],
        out_specs=(vmem, vmem),
        compiler_params=params,
        name="close",
    )(table)
    return (flux, nodal.reshape(own_nodes))


def solution(mesh):
    in_specs = (
        P("macro", "pencil", None, None),
        P("macro", "pencil", None, None),
        P("macro", None),
        P("macro"),
        P("macro", None),
        P("macro"),
        P("macro"),
    )
    out_specs = (P("macro", None), P("macro"))
    return jax.shard_map(
        on_device, mesh=mesh, in_specs=in_specs, out_specs=out_specs, check_vma=False
    )
```

```python
import math

import jax
import jax.numpy as jnp
import ml_dtypes
import numpy as np
from jax import lax
from jax.experimental import pallas as pl
from jax.experimental.pallas import tpu as pltpu
from jax.sharding import PartitionSpec as P

PHASES = 3
LANES = 128
ROWS = 8
PIECES = 4
VMEM_BYTES = 48 * 1024 * 1024
HBM_INPUTS_BYTES = 56 * 1024 * 1024


def split_table(table):
    high = table.astype(ml_dtypes.bfloat16)
    low = (table - high.astype(np.float64)).astype(ml_dtypes.bfloat16)
    return high, low


def from_right(table):
    high, low = split_table(table)
    return np.block([[high, low], [high, low]])


def from_left(table):
    high, low = split_table(table)
    return np.block([[high, high], [low, low]])


def mode_tables(width, slab):
    half = width // 2
    mode = np.arange(width)
    number = np.where(mode <= half, mode, mode - half)
    angle = 2.0 * np.pi * (number[:, None] * np.arange(width)[None, :] % width) / width
    basis = np.where((mode <= half)[:, None], np.cos(angle), np.sin(angle)) * math.sqrt(2.0 / width)
    basis[0] /= math.sqrt(2.0)
    basis[half] /= math.sqrt(2.0)
    slope = basis - np.roll(basis, 1, axis=1)
    slope[0] = 0.0
    line = 4.0 * np.sin(np.pi * number / width) ** 2
    plane = line[:, None] + line[None, :]
    rho = 1.0 + plane / 2.0 - np.sqrt(plane + plane * plane / 4.0)
    zero = plane == 0.0
    norm = np.where(zero, 0.0, 1.0 / np.where(zero, 1.0, 1.0 / rho - rho))
    scale = np.where(zero, 1.0, 1.0 / np.where(zero, 1.0, 1.0 - rho**width))
    f32 = lambda table: table.astype(np.float32)
    return dict(
        basis=basis,
        slope=slope,
        rho=f32(rho),
        norm=f32(norm),
        step=f32(rho**slab),
        chip_step=f32(rho ** (2 * slab)),
        scale=f32(scale),
    )


def halves(data):
    high = data.astype(jnp.bfloat16)
    low = (data - high.astype(jnp.float32)).astype(jnp.bfloat16)
    return high, low


def beside(data):
    return jnp.concatenate(halves(data), axis=1)


def stacked(data):
    return jnp.concatenate(halves(data), axis=0)


def product(left, right):
    return jnp.dot(left, right, preferred_element_type=jnp.float32)


def corner_mask(shape):
    row = lax.broadcasted_iota(jnp.int32, shape, 0)
    lane = lax.broadcasted_iota(jnp.int32, shape, 1)
    return (row == 0) & (lane == 0)


def analyse_kernel(
    material_hbm, ids_hbm, fiber_hbm, right_hbm, left_hbm, norm_hbm, rho_hbm,
    conduct_hbm, modes_hbm, keep_hbm, give_hbm,
    conduct_ref, modes_ref, keep_ref, give_ref, sums_ref, material_ref, ids_ref, fiber_ref, right_ref, left_ref, norm_ref, rho_ref,
    table_sems, ids_sems, fiber_sems, conduct_sems, modes_sems, tail_sems,
):
    slab, width = fiber_ref.shape[0], fiber_ref.shape[2]
    group = slab // PIECES
    odd = lax.rem(lax.axis_index("pencil"), 2) == 1

    def ids_copy(piece):
        at = pl.ds(piece * group, group)
        return pltpu.make_async_copy(ids_hbm.at[0, at], ids_ref.at[at], ids_sems.at[piece])

    def fiber_copy(piece):
        at = pl.ds(piece * group, group)
        return pltpu.make_async_copy(fiber_hbm.at[0, at], fiber_ref.at[at], fiber_sems.at[piece])

    def conduct_copy(piece):
        at = pl.ds(piece * group, group)
        return pltpu.make_async_copy(conduct_ref.at[at], conduct_hbm.at[at], conduct_sems.at[piece])

    def modes_copy(piece):
        at = pl.ds(piece * group, group)
        return pltpu.make_async_copy(modes_ref.at[at], modes_hbm.at[at], modes_sems.at[piece])

    tables = [
        pltpu.make_async_copy(source, target, table_sems.at[index])
        for index, (source, target) in enumerate(
            (
                (material_hbm, material_ref),
                (right_hbm, right_ref),
                (left_hbm, left_ref),
                (norm_hbm, norm_ref),
                (rho_hbm, rho_ref),
            )
        )
    ]
    tables[0].start()
    ids_copy(0).start()
    fiber_copy(0).start()
    for copy in tables[1:]:
        copy.start()
    for piece in range(1, PIECES):
        ids_copy(piece).start()
        fiber_copy(piece).start()
    sums_ref[...] = jnp.zeros_like(sums_ref)
    tables[0].wait()

    def along_z(piece):
        if piece == 0:
            for each in range(PIECES):
                ids_copy(each).wait()
                fiber_copy(each).wait()
            for copy in tables[1:]:
                copy.wait()
        planes = []
        for part in range(group):
            x = group * piece + part
            ids = ids_ref[x]
            conduct = jnp.where(
                ids == 0, material_ref[0, 0], jnp.where(ids == 1, material_ref[0, 1], material_ref[0, 2])
            )
            conduct = conduct * fiber_ref[x]
            conduct_ref[x] = conduct
            tiles = conduct.reshape(width // ROWS, ROWS, width)
            sums_ref[0] += jnp.sum(tiles, axis=0)
            sums_ref[1] += jnp.sum(tiles * tiles, axis=0)
            planes.append(beside(conduct))
        conduct_copy(piece).start()
        lines = product(jnp.concatenate(planes, axis=0), right_ref[...])
        return lines[:, :width] + lines[:, width:]

    def along_y(piece, lines):
        for part in range(0, group, 2):
            pair = jnp.concatenate(
                [lines[part * width : (part + 1) * width], lines[(part + 1) * width : (part + 2) * width]], axis=1
            )
            modes = product(left_ref[...], stacked(pair))
            modes = modes[:width] + modes[width:]
            modes_ref[group * piece + part] = modes[:, :width]
            modes_ref[group * piece + part + 1] = modes[:, width:]
        modes_copy(piece).start()

    lines = along_z(0)
    for piece in range(1, PIECES):
        ahead = along_z(piece)
        along_y(piece - 1, lines)
        lines = ahead
    along_y(PIECES - 1, lines)
    total = jnp.sum(sums_ref[0])
    total_square = jnp.sum(sums_ref[1])
    rho = rho_ref[...]
    right = modes_ref[0]
    left = modes_ref[slab - 1]
    for x in range(1, slab):
        right = modes_ref[x] + rho * right
        left = modes_ref[slab - 1 - x] + rho * left
    corner = corner_mask(right.shape)
    norm = norm_ref[...]
    right = jnp.where(corner, total, right * norm)
    left = jnp.where(corner, total_square, left * norm)
    tails = [
        pltpu.make_async_copy(give_ref, give_hbm, tail_sems.at[0]),
        pltpu.make_async_copy(keep_ref, keep_hbm, tail_sems.at[1]),
    ]
    give_ref[...] = jnp.where(odd, right, left)
    tails[0].start()
    keep_ref[...] = jnp.where(odd, left, right)
    tails[1].start()
    for copy in tails:
        copy.wait()
    for piece in range(PIECES):
        conduct_copy(piece).wait()
        modes_copy(piece).wait()


def moments_kernel(
    conduct_ref, modes_ref, own_ref, other_ref, extra_ref, rho_ref,
    right_basis_ref, right_slope_ref, left_basis_ref, left_slope_ref,
    out_ref, potential_ref, rise_ref, px_ref, py_ref, pz_ref, lines_ref,
):
    slab, width = conduct_ref.shape[0], conduct_ref.shape[2]
    volume = float(width**3)
    pencil = lax.axis_index("pencil")
    odd = lax.rem(pencil, 2) == 1

    corner = corner_mask((width, width))
    first_plane = jnp.where(odd, other_ref[...], own_ref[...])
    second_plane = jnp.where(odd, own_ref[...], other_ref[...])
    first = jnp.sum(jnp.where(corner, first_plane, 0.0)[:ROWS])
    second = jnp.sum(jnp.where(corner, second_plane, 0.0)[:ROWS])
    mean = first / volume
    rho = rho_ref[...]
    behind = jnp.where(corner, 0.0, second_plane)
    potential_ref[slab] = behind
    behind = rho * behind
    potential_ref[slab - 1] = behind
    for x in range(slab - 2, -1, -1):
        behind = rho * (modes_ref[x + 1] + behind)
        potential_ref[x] = behind
    ahead = jnp.where(corner, 0.0, first_plane)
    last = ahead + rho * (modes_ref[0] + behind)
    for x in range(slab + 1):
        ahead = rho * ahead
        if x < slab:
            ahead = ahead + modes_ref[x]
        here = ahead + potential_ref[x]
        potential_ref[x] = here
        rise_ref[x] = here - last
        last = here
    potential_ref[slab + 1] = last
    rise_ref[slab + 1] = last

    def put(ref, x, plane):
        ref[x, :width] = plane
        ref[x, width:] = plane[:ROWS]

    def along_z(pair):
        planes = [2 * pair, 2 * pair + 1]
        along = jnp.concatenate([beside(potential_ref[x]) for x in planes], axis=0)
        rise = product(jnp.concatenate([beside(rise_ref[x]) for x in planes], axis=0), right_basis_ref[...])
        slope = product(along, right_slope_ref[...])
        plain = product(along, right_basis_ref[...])
        for place, lines in enumerate((slope, rise, plain)):
            high, low = halves(lines[:, :width] + lines[:, width:])
            for part in range(2):
                rows = slice(part * width, (part + 1) * width)
                lanes = pl.ds((2 * part + place if place < 2 else 4 + part) * width, width)
                lines_ref[:width, lanes] = high[rows]
                lines_ref[width:, lanes] = low[rows]

    def along_y(pair):
        third = product(left_slope_ref[...], lines_ref[:, 4 * width :])
        third = third[:width] + third[width:]
        for part in range(2):
            both = product(left_basis_ref[...], lines_ref[:, 2 * part * width : 2 * (part + 1) * width])
            both = both[:width] + both[width:]
            put(pz_ref, 2 * pair + part, both[:, :width])
            put(px_ref, 2 * pair + part, both[:, width:])
            put(py_ref, 2 * pair + part, third[:, part * width : (part + 1) * width])

    pairs = slab // 2 + 1

    def differences(x, totals):
        totals = list(totals)
        for chunk in range(width // ROWS):
            at = pl.ds(chunk * ROWS, ROWS)
            down = pl.ds(chunk * ROWS + 1, ROWS)
            conduct = conduct_ref[x, at]
            px, py, pz = px_ref[x, at], py_ref[x, at], pz_ref[x, at]
            turn = lambda field: pltpu.roll(field, width - 1, 1) - field
            e_yx, e_zx = px_ref[x, down] - px, turn(px)
            e_xy, e_yy, e_zy = py_ref[x + 1, at] - py, py_ref[x, down] - py, turn(py)
            e_xz, e_yz, e_zz = pz_ref[x + 1, at] - pz, pz_ref[x, down] - pz, turn(pz)
            e_xx = (mean - conduct) - (e_yy + e_zz)
            e = ((e_xx, e_yx, e_zx), (e_xy, e_yy, e_zy), (e_xz, e_yz, e_zz))
            at_entry = 0
            for i in range(3):
                for j in range(i, 3):
                    term = e[i][0] * e[j][0] + e[i][1] * e[j][1] + e[i][2] * e[j][2]
                    totals[at_entry] = totals[at_entry] + term
                    totals[6 + at_entry] = totals[6 + at_entry] + conduct * term
                    at_entry += 1
        return tuple(totals)

    nothing = jnp.zeros((ROWS, width), jnp.float32)
    totals = (nothing,) * 12
    for step in range(pairs + 2):
        if step >= 3:
            totals = differences(2 * (step - 3), totals)
        if 1 <= step <= pairs:
            along_y(step - 1)
        if step >= 3:
            totals = differences(2 * (step - 3) + 1, totals)
        if step < pairs:
            along_z(step)
    lines = [jnp.sum(total, axis=0, keepdims=True) for total in totals]
    lines = jnp.concatenate(lines + [jnp.zeros((4, width), jnp.float32)], axis=0)
    column = jnp.sum(lines, axis=1, keepdims=True)
    row = lax.broadcasted_iota(jnp.int32, (16, width), 0)
    lane = lax.broadcasted_iota(jnp.int32, (16, width), 1)
    once = jnp.where(pencil == 0, 1.0, 0.0)
    column = jnp.where(row == 12, first * once, jnp.where(row == 13, second * once, column))
    out_ref[...] = jnp.sum(jnp.where(row == lane, column, 0.0), axis=0, keepdims=True) + extra_ref[...] * once


def close_kernel(nodes_own, volume, table_ref, flux_ref, nodal_ref):
    points = table_ref.shape[0]
    macro = lax.axis_index("macro")
    table = table_ref[...]
    lane = lax.broadcasted_iota(jnp.int32, (points, LANES), 1)
    row = lax.broadcasted_iota(jnp.int32, (points, LANES), 0)
    column = lambda index: table[:, index : index + 1]

    temperature = jnp.zeros((points, LANES), jnp.float32)
    node_of = jnp.zeros((points, LANES), jnp.float32)
    mine = (macro * nodes_own + lane).astype(jnp.float32)
    for node in range(nodes_own):
        at = row * nodes_own + node
        temperature = jnp.where(lane == at, column(16 + node), temperature)
        node_of = jnp.where(column(16 + nodes_own + node) == mine, at.astype(jnp.float32), node_of)
    temperature = jnp.sum(temperature, axis=0, keepdims=True)
    node_of = jnp.sum(node_of, axis=0, keepdims=True)
    node_of = jnp.where(lane[:1] < nodes_own, node_of, -1.0)
    assign = column(16 + 2 * nodes_own)
    corners = [column(17 + 2 * nodes_own + corner) for corner in range(8)]
    theta = []
    for corner in range(8):
        pick = lane.astype(jnp.float32) == corners[corner]
        theta.append(jnp.sum(jnp.where(pick, temperature, 0.0), axis=1, keepdims=True))
    sign = lambda corner, axis: 2.0 * (corner >> axis & 1) - 1.0
    gradient = [sum(sign(a, d) * theta[a] for a in range(8)) / 4.0 for d in range(3)]
    heat = sum(theta) / 8.0
    chosen = jnp.where(
        lax.broadcasted_iota(jnp.int32, (points, points), 1).astype(jnp.float32) == assign, 1.0, 0.0
    )
    high, rest = halves(table)
    low = (table - high.astype(jnp.float32) - rest.astype(jnp.float32)).astype(jnp.bfloat16)
    picked = product(chosen.astype(jnp.bfloat16), jnp.concatenate([high, rest, low], axis=1))
    moments = (picked[:, :LANES] + (picked[:, LANES : 2 * LANES] + picked[:, 2 * LANES :])) * (1.0 / volume)
    moment = lambda index: moments[:, index : index + 1]
    mean, mean_square = moment(12), moment(13)
    radiative = heat * heat * heat
    inverse_k = lax.rsqrt(mean_square + 2.0 * radiative * mean + radiative * radiative)
    order = ((0, 1, 2), (1, 3, 4), (2, 4, 5))
    flux = []
    for d in range(3):
        plain = sum(moment(order[d][j]) * gradient[j] for j in range(3))
        weighted = sum(moment(6 + order[d][j]) * gradient[j] for j in range(3))
        flux.append(
            gradient[d] * (mean + radiative)
            + weighted * (inverse_k * inverse_k)
            - plain * (inverse_k * (2.0 - radiative * inverse_k))
        )
    spread = jnp.zeros((points, LANES), jnp.float32)
    for d in range(3):
        spread = jnp.where(lane == d, flux[d], spread)
    flux_ref[...] = jnp.sum(jnp.where(row == macro, spread, 0.0), axis=0, keepdims=True)[:, :3]
    assembled = jnp.zeros((points, LANES), jnp.float32)
    for corner in range(8):
        residual = sum(sign(corner, d) * flux[d] for d in range(3)) / 4.0
        assembled = assembled + jnp.where(corners[corner] == node_of, residual, 0.0)
    nodal_ref[...] = jnp.sum(assembled, axis=0, keepdims=True)[:, :nodes_own]


def on_device(
    voxel_material_ids,
    fiber_fraction,
    material_matrix_diffusivity,
    mesh_point_thermal_state,
    element_corner_ids,
    global_entry_position,
    sample_choice_per_point,
):
    slab = fiber_fraction.shape[1]
    width = fiber_fraction.shape[3]
    volume = float(width**3)
    own_nodes = mesh_point_thermal_state.shape[0]
    pencils = lax.axis_size("pencil")
    chips = pencils // 2
    groups = lax.axis_size("macro")
    tables = mode_tables(width, slab)
    plane = jax.ShapeDtypeStruct((width, width), jnp.float32)
    block = jax.ShapeDtypeStruct((slab, width, width), jnp.float32)
    params = pltpu.CompilerParams(vmem_limit_bytes=VMEM_BYTES)
    vmem = pl.BlockSpec(memory_space=pltpu.VMEM)
    hbm = pl.BlockSpec(memory_space=pltpu.HBM)

    conduct, modes, keep, give = pl.pallas_call(
        analyse_kernel,
        out_shape=(block, block, plane, plane),
        in_specs=[hbm] * 7,
        out_specs=(hbm,) * 4,
        scratch_shapes=[
            pltpu.VMEM((slab, width, width), jnp.float32),
            pltpu.VMEM((slab, width, width), jnp.float32),
            pltpu.VMEM((width, width), jnp.float32),
            pltpu.VMEM((width, width), jnp.float32),
            pltpu.VMEM((2, ROWS, width), jnp.float32),
            pltpu.SMEM((1, PHASES), jnp.float32),
            pltpu.VMEM((slab, width, width), jnp.int32),
            pltpu.VMEM((slab, width, width), jnp.float32),
            pltpu.VMEM((2 * width, 2 * width), jnp.bfloat16),
            pltpu.VMEM((2 * width, 2 * width), jnp.bfloat16),
            pltpu.VMEM((width, width), jnp.float32),
            pltpu.VMEM((width, width), jnp.float32),
            pltpu.SemaphoreType.DMA((5,)),
            pltpu.SemaphoreType.DMA((PIECES,)),
            pltpu.SemaphoreType.DMA((PIECES,)),
            pltpu.SemaphoreType.DMA((PIECES,)),
            pltpu.SemaphoreType.DMA((PIECES,)),
            pltpu.SemaphoreType.DMA((2,)),
        ],
        compiler_params=pltpu.CompilerParams(vmem_limit_bytes=HBM_INPUTS_BYTES),
        name="analyse",
    )(
        material_matrix_diffusivity,
        voxel_material_ids,
        fiber_fraction,
        from_right(tables["basis"].T),
        from_left(tables["basis"]),
        tables["norm"],
        tables["rho"],
    )

    swap = [(i, i ^ 1) for i in range(pencils)]

    def from_chip(array, away):
        perm = [(i, (i + (2 * away if i % 2 == 0 else -2 * away)) % pencils) for i in range(pencils)]
        return lax.ppermute(array, "pencil", perm)

    step, chip_step = tables["step"], tables["chip_step"]
    chip = lax.ppermute(give, "pencil", swap) + lax.optimization_barrier(step * keep)
    chip, keep, modes, temperature, entry, assign, corners = lax.optimization_barrier(
        (chip, keep, modes, mesh_point_thermal_state, global_entry_position, sample_choice_per_point, element_corner_ids)
    )
    modes = lax.optimization_barrier(modes * tables["norm"])
    kept = lax.optimization_barrier(jnp.where(corner_mask((width, width)), 0.0, keep))
    extra = jnp.concatenate(
        [
            temperature,
            entry.astype(jnp.float32),
            assign.astype(jnp.float32),
            corners.reshape(-1).astype(jnp.float32),
        ]
    )
    extra = jnp.pad(extra, (16, LANES - 16 - extra.shape[0])).reshape(1, LANES)
    half = chips // 2
    powers = [tables["scale"], tables["scale"] * chip_step]
    while len(powers) < chips:
        powers.append(powers[-1] * chip_step)
    own = lax.optimization_barrier(powers[half - 1] * from_chip(chip, half) + powers[-1] * chip)
    for away in range(1, chips):
        if away != half:
            own = lax.optimization_barrier(own + powers[away - 1] * from_chip(chip, away))
    other = lax.ppermute(kept + step * own, "pencil", swap)

    field = (slab + 2, width, width)
    padded = (slab + 2, width + ROWS, width)
    moments = pl.pallas_call(
        moments_kernel,
        out_shape=jax.ShapeDtypeStruct((1, LANES), jnp.float32),
        in_specs=[vmem] * 10,
        out_specs=vmem,
        scratch_shapes=[pltpu.VMEM(s, jnp.float32) for s in (field, field, padded, padded, padded)]
        + [pltpu.VMEM((2 * width, 6 * width), jnp.bfloat16)],
        compiler_params=params,
        name="moments",
    )(
        conduct,
        modes,
        own,
        other,
        extra,
        tables["rho"],
        from_right(tables["basis"]),
        from_right(tables["slope"]),
        from_left(tables["basis"].T),
        from_left(tables["slope"].T),
    )

    table = jnp.broadcast_to(moments, (pencils, LANES))
    table = jnp.sum(lax.all_to_all(table, "pencil", 0, 0, tiled=True), axis=0, keepdims=True)
    table = lax.all_to_all(jnp.broadcast_to(table, (groups, LANES)), "macro", 0, 0, tiled=True)
    flux, nodal = pl.pallas_call(
        lambda *refs: close_kernel(own_nodes, volume, *refs),
        out_shape=(
            jax.ShapeDtypeStruct((1, 3), jnp.float32),
            jax.ShapeDtypeStruct((1, own_nodes), jnp.float32),
        ),
        in_specs=[vmem],
        out_specs=(vmem, vmem),
        compiler_params=params,
        name="close",
    )(table)
    return (flux, nodal.reshape(own_nodes))


def solution(mesh):
    in_specs = (
        P("macro", "pencil", None, None),
        P("macro", "pencil", None, None),
        P("macro", None),
        P("macro"),
        P("macro", None),
        P("macro"),
        P("macro"),
    )
    out_specs = (P("macro", None), P("macro"))
    return jax.shard_map(
        on_device, mesh=mesh, in_specs=in_specs, out_specs=out_specs, check_vma=False
    )
```

```python
import math

import jax
import jax.numpy as jnp
import ml_dtypes
import numpy as np
from jax import lax
from jax.experimental import pallas as pl
from jax.experimental.pallas import tpu as pltpu
from jax.sharding import PartitionSpec as P

PHASES = 3
LANES = 128
ROWS = 8
PIECES = 4
VMEM_BYTES = 48 * 1024 * 1024
HBM_INPUTS_BYTES = 56 * 1024 * 1024


def split_table(table):
    high = table.astype(ml_dtypes.bfloat16)
    low = (table - high.astype(np.float64)).astype(ml_dtypes.bfloat16)
    return high, low


def from_right(table):
    high, low = split_table(table)
    return np.block([[high, low], [high, low]])


def from_left(table):
    high, low = split_table(table)
    return np.block([[high, high], [low, low]])


def mode_tables(width, slab):
    half = width // 2
    mode = np.arange(width)
    number = np.where(mode <= half, mode, mode - half)
    angle = 2.0 * np.pi * (number[:, None] * np.arange(width)[None, :] % width) / width
    basis = np.where((mode <= half)[:, None], np.cos(angle), np.sin(angle)) * math.sqrt(2.0 / width)
    basis[0] /= math.sqrt(2.0)
    basis[half] /= math.sqrt(2.0)
    slope = basis - np.roll(basis, 1, axis=1)
    slope[0] = 0.0
    line = 4.0 * np.sin(np.pi * number / width) ** 2
    plane = line[:, None] + line[None, :]
    rho = 1.0 + plane / 2.0 - np.sqrt(plane + plane * plane / 4.0)
    zero = plane == 0.0
    norm = np.where(zero, 0.0, 1.0 / np.where(zero, 1.0, 1.0 / rho - rho))
    scale = np.where(zero, 1.0, 1.0 / np.where(zero, 1.0, 1.0 - rho**width))
    f32 = lambda table: table.astype(np.float32)
    return dict(
        basis=basis,
        slope=slope,
        rho=f32(rho),
        norm=f32(norm),
        step=f32(rho**slab),
        chip_step=f32(rho ** (2 * slab)),
        scale=f32(scale),
    )


def halves(data):
    high = data.astype(jnp.bfloat16)
    low = (data - high.astype(jnp.float32)).astype(jnp.bfloat16)
    return high, low


def beside(data):
    return jnp.concatenate(halves(data), axis=1)


def stacked(data):
    return jnp.concatenate(halves(data), axis=0)


def product(left, right):
    return jnp.dot(left, right, preferred_element_type=jnp.float32)


def corner_mask(shape):
    row = lax.broadcasted_iota(jnp.int32, shape, 0)
    lane = lax.broadcasted_iota(jnp.int32, shape, 1)
    return (row == 0) & (lane == 0)


def analyse_kernel(
    material_hbm, ids_hbm, fiber_hbm, right_hbm, left_hbm, norm_hbm, rho_hbm,
    conduct_hbm, modes_hbm, keep_hbm, give_hbm,
    conduct_ref, modes_ref, keep_ref, give_ref, sums_ref, material_ref, ids_ref, fiber_ref, right_ref, left_ref, norm_ref, rho_ref,
    table_sems, ids_sems, fiber_sems, conduct_sems, modes_sems, tail_sems,
):
    slab, width = fiber_ref.shape[0], fiber_ref.shape[2]
    group = slab // PIECES
    odd = lax.rem(lax.axis_index("pencil"), 2) == 1

    def ids_copy(piece):
        at = pl.ds(piece * group, group)
        return pltpu.make_async_copy(ids_hbm.at[0, at], ids_ref.at[at], ids_sems.at[piece])

    def fiber_copy(piece):
        at = pl.ds(piece * group, group)
        return pltpu.make_async_copy(fiber_hbm.at[0, at], fiber_ref.at[at], fiber_sems.at[piece])

    def conduct_copy(piece):
        at = pl.ds(piece * group, group)
        return pltpu.make_async_copy(conduct_ref.at[at], conduct_hbm.at[at], conduct_sems.at[piece])

    def modes_copy(piece):
        at = pl.ds(piece * group, group)
        return pltpu.make_async_copy(modes_ref.at[at], modes_hbm.at[at], modes_sems.at[piece])

    tables = [
        pltpu.make_async_copy(source, target, table_sems.at[index])
        for index, (source, target) in enumerate(
            (
                (material_hbm, material_ref),
                (right_hbm, right_ref),
                (left_hbm, left_ref),
                (norm_hbm, norm_ref),
                (rho_hbm, rho_ref),
            )
        )
    ]
    tables[0].start()
    ids_copy(0).start()
    fiber_copy(0).start()
    for copy in tables[1:]:
        copy.start()
    for piece in range(1, PIECES):
        ids_copy(piece).start()
        fiber_copy(piece).start()
    sums_ref[...] = jnp.zeros_like(sums_ref)
    tables[0].wait()

    def along_z(piece):
        if piece == 0:
            for each in range(PIECES):
                ids_copy(each).wait()
                fiber_copy(each).wait()
            for copy in tables[1:]:
                copy.wait()
        planes = []
        for part in range(group):
            x = group * piece + part
            ids = ids_ref[x]
            conduct = jnp.where(
                ids == 0, material_ref[0, 0], jnp.where(ids == 1, material_ref[0, 1], material_ref[0, 2])
            )
            conduct = conduct * fiber_ref[x]
            conduct_ref[x] = conduct
            tiles = conduct.reshape(width // ROWS, ROWS, width)
            sums_ref[0] += jnp.sum(tiles, axis=0)
            sums_ref[1] += jnp.sum(tiles * tiles, axis=0)
            planes.append(beside(conduct))
        conduct_copy(piece).start()
        lines = product(jnp.concatenate(planes, axis=0), right_ref[...])
        return lines[:, :width] + lines[:, width:]

    def along_y(piece, lines):
        for part in range(0, group, 2):
            pair = jnp.concatenate(
                [lines[part * width : (part + 1) * width], lines[(part + 1) * width : (part + 2) * width]], axis=1
            )
            modes = product(left_ref[...], stacked(pair))
            modes = modes[:width] + modes[width:]
            modes_ref[group * piece + part] = modes[:, :width]
            modes_ref[group * piece + part + 1] = modes[:, width:]
        modes_copy(piece).start()

    lines = along_z(0)
    for piece in range(1, PIECES):
        ahead = along_z(piece)
        along_y(piece - 1, lines)
        lines = ahead
    along_y(PIECES - 1, lines)
    total = jnp.sum(sums_ref[0])
    total_square = jnp.sum(sums_ref[1])
    rho = rho_ref[...]
    right = modes_ref[0]
    left = modes_ref[slab - 1]
    for x in range(1, slab):
        right = modes_ref[x] + rho * right
        left = modes_ref[slab - 1 - x] + rho * left
    corner = corner_mask(right.shape)
    norm = norm_ref[...]
    right = jnp.where(corner, total, right * norm)
    left = jnp.where(corner, total_square, left * norm)
    tails = [
        pltpu.make_async_copy(give_ref, give_hbm, tail_sems.at[0]),
        pltpu.make_async_copy(keep_ref, keep_hbm, tail_sems.at[1]),
    ]
    give_ref[...] = jnp.where(odd, right, left)
    tails[0].start()
    keep_ref[...] = jnp.where(odd, left, right)
    tails[1].start()
    for copy in tails:
        copy.wait()
    for piece in range(PIECES):
        conduct_copy(piece).wait()
        modes_copy(piece).wait()


def moments_kernel(
    conduct_ref, modes_ref, own_ref, other_ref, extra_ref, rho_ref,
    right_basis_ref, right_slope_ref, left_basis_ref, left_slope_ref,
    out_ref, potential_ref, rise_ref, px_ref, py_ref, pz_ref, lines_ref,
):
    slab, width = conduct_ref.shape[0], conduct_ref.shape[2]
    volume = float(width**3)
    pencil = lax.axis_index("pencil")
    odd = lax.rem(pencil, 2) == 1

    corner = corner_mask((width, width))
    first_plane = jnp.where(odd, other_ref[...], own_ref[...])
    second_plane = jnp.where(odd, own_ref[...], other_ref[...])
    first = jnp.sum(jnp.where(corner, first_plane, 0.0)[:ROWS])
    second = jnp.sum(jnp.where(corner, second_plane, 0.0)[:ROWS])
    mean = first / volume
    rho = rho_ref[...]
    behind = jnp.where(corner, 0.0, second_plane)
    potential_ref[slab] = behind
    behind = rho * behind
    potential_ref[slab - 1] = behind
    for x in range(slab - 2, -1, -1):
        behind = rho * (modes_ref[x + 1] + behind)
        potential_ref[x] = behind
    ahead = jnp.where(corner, 0.0, first_plane)
    last = ahead + rho * (modes_ref[0] + behind)
    for x in range(slab + 1):
        ahead = rho * ahead
        if x < slab:
            ahead = ahead + modes_ref[x]
        here = ahead + potential_ref[x]
        potential_ref[x] = here
        rise_ref[x] = here - last
        last = here
    potential_ref[slab + 1] = last
    rise_ref[slab + 1] = last

    def put(ref, x, plane):
        ref[x, :width] = plane
        ref[x, width:] = plane[:ROWS]

    def along_z(pair):
        planes = [2 * pair, 2 * pair + 1]
        along = jnp.concatenate([beside(potential_ref[x]) for x in planes], axis=0)
        rise = product(jnp.concatenate([beside(rise_ref[x]) for x in planes], axis=0), right_basis_ref[...])
        slope = product(along, right_slope_ref[...])
        plain = product(along, right_basis_ref[...])
        for place, lines in enumerate((slope, rise, plain)):
            high, low = halves(lines[:, :width] + lines[:, width:])
            for part in range(2):
                rows = slice(part * width, (part + 1) * width)
                lanes = pl.ds((2 * part + place if place < 2 else 4 + part) * width, width)
                lines_ref[:width, lanes] = high[rows]
                lines_ref[width:, lanes] = low[rows]

    def along_y(pair):
        third = product(left_slope_ref[...], lines_ref[:, 4 * width :])
        third = third[:width] + third[width:]
        for part in range(2):
            both = product(left_basis_ref[...], lines_ref[:, 2 * part * width : 2 * (part + 1) * width])
            both = both[:width] + both[width:]
            put(pz_ref, 2 * pair + part, both[:, :width])
            put(px_ref, 2 * pair + part, both[:, width:])
            put(py_ref, 2 * pair + part, third[:, part * width : (part + 1) * width])

    pairs = slab // 2 + 1

    def differences(pair, totals):
        totals = list(totals)
        for place in range(2 * (width // ROWS)):
            x = 2 * pair + place // (width // ROWS)
            chunk = place % (width // ROWS)
            at = pl.ds(chunk * ROWS, ROWS)
            down = pl.ds(chunk * ROWS + 1, ROWS)
            conduct = conduct_ref[x, at]
            px, py, pz = px_ref[x, at], py_ref[x, at], pz_ref[x, at]
            turn = lambda field: pltpu.roll(field, width - 1, 1) - field
            e_yx, e_zx = px_ref[x, down] - px, turn(px)
            e_xy, e_yy, e_zy = py_ref[x + 1, at] - py, py_ref[x, down] - py, turn(py)
            e_xz, e_yz, e_zz = pz_ref[x + 1, at] - pz, pz_ref[x, down] - pz, turn(pz)
            e_xx = (mean - conduct) - (e_yy + e_zz)
            e = ((e_xx, e_yx, e_zx), (e_xy, e_yy, e_zy), (e_xz, e_yz, e_zz))
            at_entry = 0
            for i in range(3):
                for j in range(i, 3):
                    term = e[i][0] * e[j][0] + e[i][1] * e[j][1] + e[i][2] * e[j][2]
                    totals[at_entry] = totals[at_entry] + term
                    totals[6 + at_entry] = totals[6 + at_entry] + conduct * term
                    at_entry += 1
        return tuple(totals)

    nothing = jnp.zeros((ROWS, width), jnp.float32)
    totals = (nothing,) * 12
    for step in range(pairs + 2):
        if 1 <= step <= pairs:
            along_y(step - 1)
        if step >= 3:
            totals = differences(step - 3, totals)
        if step < pairs:
            along_z(step)
    lines = [jnp.sum(total, axis=0, keepdims=True) for total in totals]
    lines = jnp.concatenate(lines + [jnp.zeros((4, width), jnp.float32)], axis=0)
    column = jnp.sum(lines, axis=1, keepdims=True)
    row = lax.broadcasted_iota(jnp.int32, (16, width), 0)
    lane = lax.broadcasted_iota(jnp.int32, (16, width), 1)
    once = jnp.where(pencil == 0, 1.0, 0.0)
    column = jnp.where(row == 12, first * once, jnp.where(row == 13, second * once, column))
    out_ref[...] = jnp.sum(jnp.where(row == lane, column, 0.0), axis=0, keepdims=True) + extra_ref[...] * once


def close_kernel(nodes_own, volume, table_ref, flux_ref, nodal_ref):
    points = table_ref.shape[0]
    macro = lax.axis_index("macro")
    table = table_ref[...]
    lane = lax.broadcasted_iota(jnp.int32, (points, LANES), 1)
    row = lax.broadcasted_iota(jnp.int32, (points, LANES), 0)
    column = lambda index: table[:, index : index + 1]

    temperature = jnp.zeros((points, LANES), jnp.float32)
    node_of = jnp.zeros((points, LANES), jnp.float32)
    mine = (macro * nodes_own + lane).astype(jnp.float32)
    for node in range(nodes_own):
        at = row * nodes_own + node
        temperature = jnp.where(lane == at, column(16 + node), temperature)
        node_of = jnp.where(column(16 + nodes_own + node) == mine, at.astype(jnp.float32), node_of)
    temperature = jnp.sum(temperature, axis=0, keepdims=True)
    node_of = jnp.sum(node_of, axis=0, keepdims=True)
    node_of = jnp.where(lane[:1] < nodes_own, node_of, -1.0)
    assign = column(16 + 2 * nodes_own)
    corners = [column(17 + 2 * nodes_own + corner) for corner in range(8)]
    theta = []
    for corner in range(8):
        pick = lane.astype(jnp.float32) == corners[corner]
        theta.append(jnp.sum(jnp.where(pick, temperature, 0.0), axis=1, keepdims=True))
    sign = lambda corner, axis: 2.0 * (corner >> axis & 1) - 1.0
    gradient = [sum(sign(a, d) * theta[a] for a in range(8)) / 4.0 for d in range(3)]
    heat = sum(theta) / 8.0
    chosen = jnp.where(
        lax.broadcasted_iota(jnp.int32, (points, points), 1).astype(jnp.float32) == assign, 1.0, 0.0
    )
    high, rest = halves(table)
    low = (table - high.astype(jnp.float32) - rest.astype(jnp.float32)).astype(jnp.bfloat16)
    picked = product(chosen.astype(jnp.bfloat16), jnp.concatenate([high, rest, low], axis=1))
    moments = (picked[:, :LANES] + (picked[:, LANES : 2 * LANES] + picked[:, 2 * LANES :])) * (1.0 / volume)
    moment = lambda index: moments[:, index : index + 1]
    mean, mean_square = moment(12), moment(13)
    radiative = heat * heat * heat
    inverse_k = lax.rsqrt(mean_square + 2.0 * radiative * mean + radiative * radiative)
    order = ((0, 1, 2), (1, 3, 4), (2, 4, 5))
    flux = []
    for d in range(3):
        plain = sum(moment(order[d][j]) * gradient[j] for j in range(3))
        weighted = sum(moment(6 + order[d][j]) * gradient[j] for j in range(3))
        flux.append(
            gradient[d] * (mean + radiative)
            + weighted * (inverse_k * inverse_k)
            - plain * (inverse_k * (2.0 - radiative * inverse_k))
        )
    spread = jnp.zeros((points, LANES), jnp.float32)
    for d in range(3):
        spread = jnp.where(lane == d, flux[d], spread)
    flux_ref[...] = jnp.sum(jnp.where(row == macro, spread, 0.0), axis=0, keepdims=True)[:, :3]
    assembled = jnp.zeros((points, LANES), jnp.float32)
    for corner in range(8):
        residual = sum(sign(corner, d) * flux[d] for d in range(3)) / 4.0
        assembled = assembled + jnp.where(corners[corner] == node_of, residual, 0.0)
    nodal_ref[...] = jnp.sum(assembled, axis=0, keepdims=True)[:, :nodes_own]


def on_device(
    voxel_material_ids,
    fiber_fraction,
    material_matrix_diffusivity,
    mesh_point_thermal_state,
    element_corner_ids,
    global_entry_position,
    sample_choice_per_point,
):
    slab = fiber_fraction.shape[1]
    width = fiber_fraction.shape[3]
    volume = float(width**3)
    own_nodes = mesh_point_thermal_state.shape[0]
    pencils = lax.axis_size("pencil")
    chips = pencils // 2
    groups = lax.axis_size("macro")
    tables = mode_tables(width, slab)
    plane = jax.ShapeDtypeStruct((width, width), jnp.float32)
    block = jax.ShapeDtypeStruct((slab, width, width), jnp.float32)
    params = pltpu.CompilerParams(vmem_limit_bytes=VMEM_BYTES)
    vmem = pl.BlockSpec(memory_space=pltpu.VMEM)
    hbm = pl.BlockSpec(memory_space=pltpu.HBM)

    conduct, modes, keep, give = pl.pallas_call(
        analyse_kernel,
        out_shape=(block, block, plane, plane),
        in_specs=[hbm] * 7,
        out_specs=(hbm,) * 4,
        scratch_shapes=[
            pltpu.VMEM((slab, width, width), jnp.float32),
            pltpu.VMEM((slab, width, width), jnp.float32),
            pltpu.VMEM((width, width), jnp.float32),
            pltpu.VMEM((width, width), jnp.float32),
            pltpu.VMEM((2, ROWS, width), jnp.float32),
            pltpu.SMEM((1, PHASES), jnp.float32),
            pltpu.VMEM((slab, width, width), jnp.int32),
            pltpu.VMEM((slab, width, width), jnp.float32),
            pltpu.VMEM((2 * width, 2 * width), jnp.bfloat16),
            pltpu.VMEM((2 * width, 2 * width), jnp.bfloat16),
            pltpu.VMEM((width, width), jnp.float32),
            pltpu.VMEM((width, width), jnp.float32),
            pltpu.SemaphoreType.DMA((5,)),
            pltpu.SemaphoreType.DMA((PIECES,)),
            pltpu.SemaphoreType.DMA((PIECES,)),
            pltpu.SemaphoreType.DMA((PIECES,)),
            pltpu.SemaphoreType.DMA((PIECES,)),
            pltpu.SemaphoreType.DMA((2,)),
        ],
        compiler_params=pltpu.CompilerParams(vmem_limit_bytes=HBM_INPUTS_BYTES),
        name="analyse",
    )(
        material_matrix_diffusivity,
        voxel_material_ids,
        fiber_fraction,
        from_right(tables["basis"].T),
        from_left(tables["basis"]),
        tables["norm"],
        tables["rho"],
    )

    swap = [(i, i ^ 1) for i in range(pencils)]

    def from_chip(array, away):
        perm = [(i, (i + (2 * away if i % 2 == 0 else -2 * away)) % pencils) for i in range(pencils)]
        return lax.ppermute(array, "pencil", perm)

    step, chip_step = tables["step"], tables["chip_step"]
    chip = lax.ppermute(give, "pencil", swap) + lax.optimization_barrier(step * keep)
    chip, keep, modes, temperature, entry, assign, corners = lax.optimization_barrier(
        (chip, keep, modes, mesh_point_thermal_state, global_entry_position, sample_choice_per_point, element_corner_ids)
    )
    modes = lax.optimization_barrier(modes * tables["norm"])
    kept = lax.optimization_barrier(jnp.where(corner_mask((width, width)), 0.0, keep))
    extra = jnp.concatenate(
        [
            temperature,
            entry.astype(jnp.float32),
            assign.astype(jnp.float32),
            corners.reshape(-1).astype(jnp.float32),
        ]
    )
    extra = jnp.pad(extra, (16, LANES - 16 - extra.shape[0])).reshape(1, LANES)
    half = chips // 2
    powers = [tables["scale"], tables["scale"] * chip_step]
    while len(powers) < chips:
        powers.append(powers[-1] * chip_step)
    own = lax.optimization_barrier(powers[half - 1] * from_chip(chip, half) + powers[-1] * chip)
    for away in range(1, chips):
        if away != half:
            own = own + powers[away - 1] * from_chip(chip, away)
    other = lax.ppermute(kept + step * own, "pencil", swap)

    field = (slab + 2, width, width)
    padded = (slab + 2, width + ROWS, width)
    moments = pl.pallas_call(
        moments_kernel,
        out_shape=jax.ShapeDtypeStruct((1, LANES), jnp.float32),
        in_specs=[vmem] * 10,
        out_specs=vmem,
        scratch_shapes=[pltpu.VMEM(s, jnp.float32) for s in (field, field, padded, padded, padded)]
        + [pltpu.VMEM((2 * width, 6 * width), jnp.bfloat16)],
        compiler_params=params,
        name="moments",
    )(
        conduct,
        modes,
        own,
        other,
        extra,
        tables["rho"],
        from_right(tables["basis"]),
        from_right(tables["slope"]),
        from_left(tables["basis"].T),
        from_left(tables["slope"].T),
    )

    table = jnp.broadcast_to(moments, (pencils, LANES))
    table = jnp.sum(lax.all_to_all(table, "pencil", 0, 0, tiled=True), axis=0, keepdims=True)
    table = lax.all_to_all(jnp.broadcast_to(table, (groups, LANES)), "macro", 0, 0, tiled=True)
    flux, nodal = pl.pallas_call(
        lambda *refs: close_kernel(own_nodes, volume, *refs),
        out_shape=(
            jax.ShapeDtypeStruct((1, 3), jnp.float32),
            jax.ShapeDtypeStruct((1, own_nodes), jnp.float32),
        ),
        in_specs=[vmem],
        out_specs=(vmem, vmem),
        compiler_params=params,
        name="close",
    )(table)
    return (flux, nodal.reshape(own_nodes))


def solution(mesh):
    in_specs = (
        P("macro", "pencil", None, None),
        P("macro", "pencil", None, None),
        P("macro", None),
        P("macro"),
        P("macro", None),
        P("macro"),
        P("macro"),
    )
    out_specs = (P("macro", None), P("macro"))
    return jax.shard_map(
        on_device, mesh=mesh, in_specs=in_specs, out_specs=out_specs, check_vma=False
    )
```
